128 devices in a mesh: video: 2 (over z_hi), tile: 32 (over y, x, core), section: 2 (over z_lo).
Axes of the slice: x: 4, y: 4, z: 4 (z_hi: 2, z_lo: 2; z = z_hi * 2 + z_lo), core: 2. Of those that a mesh axis runs over, the one named last changes fastest.
Arguments:
- latent: float32 [4, 32, 4, 16, 256], P('video', 'tile', 'section'), may hold values from -6 to 6
- resolution: int32 [4], replicated, may hold values from 0 to 1, as said below
- frame_counts: int32 [4], replicated, may hold values from 1 to 4, as said below
- tile_rows: int32 [4, 32], replicated, may hold values from 0 to 30, as said below
- tile_cols: int32 [4, 32], replicated, may hold values from 0 to 70, as said below
- decoder_list: int32 [4, 32], replicated, may hold values from -1 to 63, as said below
- w_in: bfloat16 [432, 384], replicated, may hold values from -0.3125 to 0.3125
- b_in: float32 [384], replicated, may hold values from -4 to 4
- gain_one: float32 [384], replicated, may hold values from 0.25 to 1.75
- w_one: bfloat16 [10368, 384], replicated, may hold values from -0.0625 to 0.0625
- b_one: float32 [384], replicated, may hold values from -4 to 4
- gain_two: float32 [384], replicated, may hold values from 0.25 to 1.75
- w_two: bfloat16 [10368, 384], replicated, may hold values from -0.0625 to 0.0625
- b_two: float32 [384], replicated, may hold values from -4 to 4
Outputs:
- decoded: bfloat16 [2, 32, 4, 100, 384], P('video', 'tile', 'section')
The draws below stay inside these ranges and needn't reach their ends.
Inputs may be any that keep to these rules, and one draw needn't show every extreme that they name: `resolution`: 0 marks a 480p video, 1 a 720p one; both occur in every draw. `frame_counts`: frames at or after this count are not part of the video. `tile_rows`: a multiple of 10; a video of resolution r has its first (1 + r) * 8 slots live, placed on distinct tiles of a grid of 2 + 2 r rows and 8 columns of tiles; other slots hold 0. `tile_cols`: a multiple of 10, on the same grid; other slots hold 0. `decoder_list`: the decoder of a live slot, -1 for the other slots; no decoder is named twice.
All inputs are finite; a program needn't handle non-finite values.
Results may differ from the reference program's by a relative error of at most 0.0051.
Values may be sent and summed in bfloat16 or wider, within the bound.
No kernel may reach another device: no remote copies, remote signals or barrier semaphores. Data moves between devices by JAX's collectives and lax.ppermute only.
A program may use at most 128 MiB of HBM per device.

```python
import jax
import jax.numpy as jnp
from jax import lax

ZC = 16
CH = 384
EXT = 16
TS = 10
FRAMES = 4
VIDEOS = 4
DECODERS = 64
LIVE_LOW = 8
GRID_COLS = 8
N_VIDEO = 2
N_TILE = 32


def layout_draw(key):
    res_key, first_key, second_key, order_key, decoder_key = jax.random.split(key, 5)
    resolved = jax.random.randint(res_key, (VIDEOS,), 0, 2)
    first_video = jax.random.randint(first_key, (), 0, VIDEOS)
    second_video = (first_video + jax.random.randint(second_key, (), 1, VIDEOS)) % VIDEOS
    resolved = resolved.at[first_video].set(1).at[second_video].set(0)
    slot_total = 4 * LIVE_LOW
    live_count = LIVE_LOW * (1 + resolved)
    cell_count = (2 + 2 * resolved) * GRID_COLS
    slot_iota = jnp.arange(slot_total, dtype=jnp.int32)
    alive = slot_iota[None, :] < live_count[:, None]
    usable = slot_iota[None, :] < cell_count[:, None]
    last_cell = slot_iota[None, :] == cell_count[:, None] - 1
    scores = jax.random.randint(order_key, (VIDEOS, slot_total), 0, 1 << 20) * slot_total + slot_iota[None, :]
    scores = jnp.where(last_cell, -1, scores)
    scores = jnp.where(usable, scores, (1 << 30) + slot_iota[None, :])
    placed = jnp.argsort(scores, axis=1, stable=True).astype(jnp.int32)
    row_values = jnp.where(alive, placed // GRID_COLS * TS, 0)
    col_values = jnp.where(alive, placed % GRID_COLS * TS, 0)
    order = jax.random.permutation(decoder_key, DECODERS).astype(jnp.int32)
    leading = order[0]
    order = jnp.where(order == DECODERS - 1, leading, order).at[0].set(DECODERS - 1)
    flat_alive = alive.reshape(-1)
    ranks = jnp.clip(jnp.cumsum(flat_alive.astype(jnp.int32)) - 1, 0, DECODERS - 1)
    chosen = jnp.where(flat_alive, order[ranks], -1).reshape(VIDEOS, slot_total)
    return (resolved.astype(jnp.int32), row_values.astype(jnp.int32), col_values.astype(jnp.int32), chosen.astype(jnp.int32))


def draw_resolution(key, part):
    return layout_draw(key)[0]


def draw_tile_rows(key, part):
    return layout_draw(key)[1]


def draw_tile_cols(key, part):
    return layout_draw(key)[2]


def draw_decoder_list(key, part):
    return layout_draw(key)[3]


def draw_frame_counts(key, part):
    key = jax.random.fold_in(key, 7)
    count_key, first_key, second_key = jax.random.split(key, 3)
    counts = jax.random.randint(count_key, (VIDEOS,), 1, FRAMES + 1)
    first_video = jax.random.randint(first_key, (), 0, VIDEOS)
    second_video = (first_video + jax.random.randint(second_key, (), 1, VIDEOS)) % VIDEOS
    counts = counts.at[first_video].set(FRAMES).at[second_video].set(1)
    return counts.astype(jnp.int32)


def block_levels(stream_key, extent, cuts, least, top_value):
    loudness = 1.0
    for dim, shards_of in cuts:
        draws = jax.random.uniform(jax.random.fold_in(jax.random.fold_in(stream_key, 6), dim), (shards_of,), jnp.float32, least / len(cuts), top_value / len(cuts))
        loudness = loudness * jnp.repeat(jnp.exp(draws), extent[dim] // shards_of).reshape((-1,) + (1,) * (len(extent) - 1 - dim))
    return loudness


def scatter_about(rng, extent, spread, reach, cuts=(), held_as=jnp.bfloat16):
    entries = jax.random.normal(rng, extent, jnp.float32) * spread
    if len(cuts) > 0:
        entries = block_levels(rng, extent, cuts, -0.22, 0.18) * entries
    return jnp.clip(entries, min=-reach, max=reach).astype(held_as)


def setup_inputs(seed: int = 0) -> dict:
    splits = jax.random.split(jax.random.key(seed), 15)
    return {
        "latent": scatter_about(splits[0], (VIDEOS, 4 * LIVE_LOW, FRAMES, EXT, EXT * ZC), 1.0, 6.0, ((0, 2), (1, 32), (2, 2)), jnp.float32),
        "resolution": draw_resolution(jax.random.fold_in(splits[14], 71), 0),
        "frame_counts": draw_frame_counts(jax.random.fold_in(splits[14], 71), 0),
        "tile_rows": draw_tile_rows(jax.random.fold_in(splits[14], 71), 0),
        "tile_cols": draw_tile_cols(jax.random.fold_in(splits[14], 71), 0),
        "decoder_list": draw_decoder_list(jax.random.fold_in(splits[14], 71), 0),
        "w_in": scatter_about(splits[6], (27 * ZC, CH), (27 * ZC) ** -0.5, 0.3125),
        "b_in": scatter_about(splits[7], (CH,), 0.3, 4.0, (), jnp.float32),
        "gain_one": jnp.clip(1.0 + 0.15 * jax.random.normal(splits[8], (CH,), jnp.float32), 0.25, 1.75),
        "w_one": scatter_about(splits[9], (27 * CH, CH), (27 * CH) ** -0.5, 0.0625),
        "b_one": scatter_about(splits[10], (CH,), 0.3, 4.0, (), jnp.float32),
        "gain_two": jnp.clip(1.0 + 0.15 * jax.random.normal(splits[11], (CH,), jnp.float32), 0.25, 1.75),
        "w_two": scatter_about(splits[12], (27 * CH, CH), (27 * CH) ** -0.5, 0.0625),
        "b_two": scatter_about(splits[13], (CH,), 0.3, 4.0, (), jnp.float32),
    }


def lookup_one(table, index):
    positions = jnp.arange(table.shape[0], dtype=jnp.int32)
    return jnp.sum(jnp.where(positions == index, table, 0)).astype(jnp.int32)

def inside_mask(tile_row, tile_col, resolved, margin):
    size = EXT - 2 * margin
    offsets = jnp.arange(size, dtype=jnp.int32) + margin - 3
    grid_row = tile_row + offsets
    grid_col = tile_col + offsets
    high = (2 + 2 * resolved) * TS - 3
    row_ok = (grid_row >= 0) & (grid_row < high)
    col_ok = (grid_col >= 0) & (grid_col < GRID_COLS * TS - 4)
    return (row_ok[:, None] & col_ok[None, :]).astype(jnp.float32)

def conv_valid(field, weight):
    frames = field.shape[0]
    padded = jnp.concatenate([jnp.zeros((2,) + field.shape[1:], field.dtype), field], axis=0)
    height = field.shape[1] - 2
    width_out = field.shape[2] - 2
    pieces = []
    for tap_time in range(3):
        for tap_row in range(3):
            for tap_col in range(3):
                pieces.append(padded[tap_time:tap_time + frames, tap_row:tap_row + height, tap_col:tap_col + width_out, :])
    columns = jnp.concatenate(pieces, axis=-1)
    flat = columns.reshape(frames * height * width_out, columns.shape[-1])
    result = jnp.dot(flat, weight, preferred_element_type=jnp.float32)
    return result.reshape(frames, height, width_out, weight.shape[1])

def normalize(values, gain):
    return values * lax.rsqrt(lax.optimization_barrier(jnp.mean(values * values, axis=-1, keepdims=True)) + 1e-06) * gain

def decode_tile(tile, tile_row, tile_col, resolved, counts, w_in, b_in, gain_one, w_one, b_one, gain_two, w_two, b_two):
    frames = tile.shape[0]
    field = tile.reshape(frames, EXT, EXT, ZC) * inside_mask(tile_row, tile_col, resolved, 0)[None, :, :, None]
    field = field.astype(jnp.bfloat16)
    stem = conv_valid(field, w_in) + b_in
    act_one = jax.nn.silu(normalize(stem, gain_one)) * inside_mask(tile_row, tile_col, resolved, 1)[None, :, :, None]
    act_one = act_one.astype(jnp.bfloat16)
    middle = conv_valid(act_one, w_one) + b_one
    act_two = jax.nn.silu(normalize(middle, gain_two)) * inside_mask(tile_row, tile_col, resolved, 2)[None, :, :, None]
    act_two = act_two.astype(jnp.bfloat16)
    final = conv_valid(act_two, w_two) + b_two + stem[:, 2:2 + TS, 2:2 + TS, :]
    valid = (jnp.arange(frames, dtype=jnp.int32) < counts).astype(jnp.float32)
    final = final * valid[:, None, None, None]
    return final.reshape(frames, TS * TS, CH)

def reference(latent, resolution, frame_counts, tile_rows, tile_cols, decoder_list, w_in, b_in, gain_one, w_one, b_one, gain_two, w_two, b_two):
    video_iota = jnp.broadcast_to(jnp.arange(VIDEOS, dtype=jnp.int32)[:, None], decoder_list.shape)

    def decode_one(decoder):
        matched = decoder_list == decoder
        alive = jnp.any(matched)
        which_video = jnp.sum(jnp.where(matched, video_iota, 0)).astype(jnp.int32)
        tile_row = jnp.sum(jnp.where(matched, tile_rows, 0)).astype(jnp.int32)
        tile_col = jnp.sum(jnp.where(matched, tile_cols, 0)).astype(jnp.int32)
        tile = lax.optimization_barrier(jnp.sum(jnp.where(matched[:, :, None, None, None], latent, jnp.zeros_like(latent)), axis=(0, 1)))
        resolved = lookup_one(resolution, which_video)
        counts = lookup_one(frame_counts, which_video)
        result = decode_tile(tile, tile_row, tile_col, resolved, counts, w_in, b_in, gain_one, w_one, b_one, gain_two, w_two, b_two)
        return jnp.where(alive, result, jnp.zeros_like(result)).astype(jnp.bfloat16)
    decoded = lax.map(decode_one, jnp.arange(DECODERS, dtype=jnp.int32))
    return decoded.reshape(N_VIDEO, N_TILE, FRAMES, TS * TS, CH)
```

```python
import jax
import jax.numpy as jnp
import numpy as np
from jax import lax
from jax.experimental import pallas as pl
from jax.experimental.pallas import tpu as pltpu
from jax.sharding import PartitionSpec as P

F32 = jnp.float32
BF16 = jnp.bfloat16
ZC = 16
CH = 384
EXT = 16
TS = 10
SPAN = 4
STEM = EXT - 2
MID = EXT - 4
STEM_ROWS = STEM * EXT
MID_ROWS = MID * MID
TAPS = 9 * CH


def gathers():
    one = np.zeros((25 * 16, STEM_ROWS), np.float32)
    for ry in range(5):
        for rx in range(5):
            for j in range(16):
                y, x = 3 * (j // 4) + ry, 3 * (j % 4) + rx
                one[(ry * 5 + rx) * 16 + j, x * EXT + y] = 1
    two = np.zeros((16 * 32, MID_ROWS), np.float32)
    for ry in range(4):
        for rx in range(4):
            for j in range(25):
                y, x = 2 * (j // 5) + ry, 2 * (j % 5) + rx
                two[(ry * 4 + rx) * 32 + j, ((y % 3) * 3 + x % 3) * 16 + (y // 3) * 4 + x // 3] = 1
    skip = np.zeros((4 * 32, STEM_ROWS), np.float32)
    out = np.zeros((112, 4 * 32), np.float32)
    for y in range(TS):
        for x in range(TS):
            row = ((y % 2) * 2 + x % 2) * 32 + (y // 2) * 5 + x // 2
            skip[row, (x + 2) * EXT + y + 2] = 1
            out[y * TS + x, row] = 1
    return [jnp.asarray(a, BF16) for a in (one, two, skip, out)]


def dot(a, b):
    return jnp.dot(a, b, preferred_element_type=F32)


def activate(u, gain):
    half = 0.5 * (u * lax.rsqrt(jnp.mean(u * u, axis=-1, keepdims=True) + 1e-06) * gain)
    return half + half * jnp.tanh(half)


def inside(row, col, high, wide):
    return ((row >= 0) & (row < high) & (col >= 0) & (col < wide)).astype(F32)


def decode_kernel(
    info, field, w_in, b_in, gain_one, b_one, gain_two, b_two, to_one, to_two, to_skip, to_out,
    w_one, w_two, out, lhs, act_one, act_two, skip, middle, w_one_v, w_two_v, sems,
):
    copies = []
    for n, (src, dst) in enumerate(((w_one, w_one_v), (w_two, w_two_v))):
        for step in range(3):
            tap = 2 - step if n == 0 else step
            copy = pltpu.make_async_copy(
                src.at[pl.ds(tap * TAPS, TAPS)], dst.at[pl.ds(tap * TAPS, TAPS)], sems.at[n, tap]
            )
            copy.start()
            copies.append(copy)
    row0, col0, high, wide, first = info[0], info[1], info[2], info[3], info[4]

    lane = lax.broadcasted_iota(jnp.int32, (SPAN * EXT, EXT * ZC), 1)
    line = lax.broadcasted_iota(jnp.int32, (SPAN * EXT, EXT * ZC), 0)
    cells = field[...].astype(F32) * inside(
        row0 - 3 + (line & (EXT - 1)), col0 - 3 + lane // ZC, high, wide
    )
    rolled = [
        cells,
        pltpu.roll(pltpu.roll(cells, SPAN * EXT - 1, 0), 3 * ZC, 1),
        pltpu.roll(pltpu.roll(cells, SPAN * EXT - 2, 0), 6 * ZC, 1),
    ]
    for x in range(STEM):
        at = [pltpu.roll(r, (EXT * ZC - ZC * x) % (EXT * ZC), 1) if x else r for r in rolled]
        packed = jnp.where(lane < 3 * ZC, at[0], jnp.where(lane < 6 * ZC, at[1], at[2]))
        lhs[:, x] = packed.astype(BF16).reshape(SPAN, EXT, EXT * ZC)

    pos = lax.broadcasted_iota(jnp.int32, (STEM_ROWS, 1), 0)
    mask_one = inside(row0 - 2 + (pos & (EXT - 1)), col0 - 2 + (pos >> 4), high, wide)
    for f in range(SPAN):
        stem = b_in[...]
        for dt in range(3):
            if f + dt - 2 >= 0:
                left = lhs[f + dt - 2].reshape(STEM_ROWS, EXT * ZC)[:, : 9 * ZC]
                stem = stem + dot(left, w_in[pl.ds(dt * 9 * ZC, 9 * ZC), :])
        act = activate(stem, gain_one[...]) * mask_one
        if f < 2:
            act = act * (first + f >= 0).astype(F32)
        moved = dot(to_one[...], act.astype(BF16))
        act_one[f] = moved.astype(BF16).reshape(5, 5, 16, CH)
        if f >= 2:
            coarse = stem.astype(BF16)
            fine = (stem - coarse.astype(F32)).astype(BF16)
            skip[f - 2] = dot(to_skip[...], coarse) + dot(to_skip[...], fine) + b_two[...]

    for step in range(3):
        dt = 2 - step
        copies[step].wait()
        frames = 2 + dt
        left = jnp.concatenate(
            [
                act_one[0:frames, dy : dy + 3, dx : dx + 3].reshape(frames * MID_ROWS, CH)
                for dy in range(3)
                for dx in range(3)
            ],
            axis=-1,
        )
        part = dot(left, w_one_v[pl.ds(dt * TAPS, TAPS), :])
        rows = pl.ds((SPAN - frames) * MID_ROWS, frames * MID_ROWS)
        if step == 0:
            middle[...] = part
        else:
            middle[rows, :] += part
    spot = lax.broadcasted_iota(jnp.int32, (MID_ROWS, 1), 0)
    block = spot >> 4
    block_y = (block >= 3).astype(jnp.int32) + (block >= 6).astype(jnp.int32)
    mid_y = 3 * ((spot >> 2) & 3) + block_y
    mid_x = 3 * (spot & 3) + block - 3 * block_y
    mask_two = inside(row0 - 1 + mid_y, col0 - 1 + mid_x, high, wide)
    for f in range(SPAN):
        act = activate(middle[pl.ds(f * MID_ROWS, MID_ROWS), :] + b_one[...], gain_two[...]) * mask_two
        if f < 2:
            act = act * (first + f >= 0).astype(F32)
        act_two[f] = dot(to_two[...], act.astype(BF16)).astype(BF16).reshape(4, 4, 32, CH)

    total = skip[...].reshape(2 * 128, CH)
    for dt in range(3):
        copies[3 + dt].wait()
        left = jnp.concatenate(
            [
                act_two[dt : dt + 2, dy : dy + 2, dx : dx + 2].reshape(2 * 128, CH)
                for dy in range(3)
                for dx in range(3)
            ],
            axis=-1,
        )
        total = total + dot(left, w_two_v[pl.ds(dt * TAPS, TAPS), :])
    for f in range(2):
        live = first + 2 + f < info[5]
        final = jnp.where(live, total[f * 128 : (f + 1) * 128], 0.0).astype(BF16)
        out[f] = dot(to_out[...], final)[: TS * TS].astype(BF16)


def decode(info, field, w_in, b_in, gain_one, w_one, b_one, gain_two, w_two, b_two):
    vmem = pl.BlockSpec(memory_space=pltpu.VMEM)
    hbm = pl.BlockSpec(memory_space=pl.ANY)
    row = lambda v: v.reshape(1, CH)
    return pl.pallas_call(
        decode_kernel,
        out_shape=jax.ShapeDtypeStruct((2, TS * TS, CH), BF16),
        in_specs=[pl.BlockSpec(memory_space=pltpu.SMEM)] + [vmem] * 11 + [hbm] * 2,
        out_specs=vmem,
        scratch_shapes=[
            pltpu.VMEM((SPAN, STEM, EXT, EXT * ZC), BF16),
            pltpu.VMEM((SPAN, 5, 5, 16, CH), BF16),
            pltpu.VMEM((SPAN, 4, 4, 32, CH), BF16),
            pltpu.VMEM((2, 128, CH), F32),
            pltpu.VMEM((SPAN * MID_ROWS, CH), F32),
            pltpu.VMEM((3 * TAPS, CH), BF16),
            pltpu.VMEM((3 * TAPS, CH), BF16),
            pltpu.SemaphoreType.DMA((2, 3)),
        ],
        compiler_params=pltpu.CompilerParams(vmem_limit_bytes=48 << 20),
        cost_estimate=pl.CostEstimate(
            flops=2 * 27 * CH * CH * (SPAN * MID_ROWS + 200), bytes_accessed=16 << 20, transcendentals=0
        ),
    )(
        info, field, w_in, row(b_in), row(gain_one), row(b_one), row(gain_two), row(b_two),
        *gathers(), w_one, w_two,
    )


def slot_info(resolution, frame_counts, tile_rows, tile_cols, decoder_list):
    mine = lax.axis_index("video") * lax.axis_size("tile") + lax.axis_index("tile")
    match = decoder_list == mine
    pick = lambda table: jnp.sum(jnp.where(match, table, 0))
    high = (2 + 2 * pick(jnp.broadcast_to(resolution[:, None], match.shape))) * TS - 3
    counts = pick(jnp.broadcast_to(frame_counts[:, None], match.shape))
    wide = lax.axis_size("tile") // 4 * TS - 4
    first = 2 * lax.axis_index("section") - 2
    return jnp.stack(
        [pick(tile_rows), pick(tile_cols), high, jnp.int32(wide), first, counts]
    ).astype(jnp.int32)


def local(
    latent, resolution, frame_counts, tile_rows, tile_cols, decoder_list,
    w_in, b_in, gain_one, w_one, b_one, gain_two, w_two, b_two,
):
    tile_count, video_count = lax.axis_size("tile"), lax.axis_size("video")
    slot = lax.axis_index("tile")
    own = lax.dynamic_slice(decoder_list, (2 * lax.axis_index("video"), slot), (2, 1))
    peers = jnp.arange(video_count * tile_count, dtype=jnp.int32)
    owned = latent[:, 0].reshape(2, 2 * EXT, EXT * ZC).astype(BF16)
    sent = jnp.where((peers == own[0, 0])[:, None, None], owned[0], jnp.zeros((), BF16))
    sent = jnp.where((peers == own[1, 0])[:, None, None], owned[1], sent)
    got = lax.all_to_all(sent, ("video", "tile"), split_axis=0, concat_axis=0, tiled=True)
    frames = jnp.sum(got, axis=0, dtype=F32).astype(BF16)
    earlier = lax.ppermute(frames, "section", [(0, 1)])
    field = jnp.concatenate([earlier, frames], axis=0)
    info = slot_info(resolution, frame_counts, tile_rows, tile_cols, decoder_list)
    decoded = decode(info, field, w_in, b_in, gain_one, w_one, b_one, gain_two, w_two, b_two)
    return decoded[None, None]


def solution(mesh):
    return jax.shard_map(
        local,
        mesh=mesh,
        in_specs=(P("video", "tile", "section", None, None),) + (P(),) * 13,
        out_specs=P("video", "tile", "section", None, None),
        check_vma=False,
    )
```

```python
import jax
import jax.numpy as jnp
import numpy as np
from jax import lax
from jax.experimental import pallas as pl
from jax.experimental.pallas import tpu as pltpu
from jax.sharding import PartitionSpec as P

F32 = jnp.float32
BF16 = jnp.bfloat16
ZC = 16
CH = 384
EXT = 16
TS = 10
SPAN = 4
STEM = EXT - 2
MID = EXT - 4
STEM_ROWS = STEM * EXT
MID_ROWS = MID * MID
TAPS = 9 * CH


def gathers():
    one = np.zeros((25 * 16, STEM_ROWS), np.float32)
    for ry in range(5):
        for rx in range(5):
            for j in range(16):
                y, x = 3 * (j // 4) + ry, 3 * (j % 4) + rx
                one[(ry * 5 + rx) * 16 + j, x * EXT + y] = 1
    two = np.zeros((16 * 32, MID_ROWS), np.float32)
    for ry in range(4):
        for rx in range(4):
            for j in range(25):
                y, x = 2 * (j // 5) + ry, 2 * (j % 5) + rx
                two[(ry * 4 + rx) * 32 + j, ((y % 3) * 3 + x % 3) * 16 + (y // 3) * 4 + x // 3] = 1
    skip = np.zeros((4 * 32, STEM_ROWS), np.float32)
    out = np.zeros((112, 4 * 32), np.float32)
    for y in range(TS):
        for x in range(TS):
            row = ((y % 2) * 2 + x % 2) * 32 + (y // 2) * 5 + x // 2
            skip[row, (x + 2) * EXT + y + 2] = 1
            out[y * TS + x, row] = 1
    return [jnp.asarray(a, BF16) for a in (one, two, skip, out)]


def dot(a, b):
    return jnp.dot(a, b, preferred_element_type=F32)


def activate(u, gain):
    half = 0.5 * (u * lax.rsqrt(jnp.mean(u * u, axis=-1, keepdims=True) + 1e-06) * gain)
    return half + half * jnp.tanh(half)


def inside(row, col, high, wide):
    return ((row >= 0) & (row < high) & (col >= 0) & (col < wide)).astype(F32)


def decode_kernel(
    info, here, across, far, vectors, w_in_h, to_one_h, to_two_h, to_skip_h, to_out_h, w_one, w_two, out,
    w_in, to_one, to_two, to_skip, to_out, lhs, act_one, act_two, skip, middle, w_one_v, w_two_v, small, sems,
):
    tables = []
    for n, (src, dst) in enumerate(
        ((w_in_h, w_in), (to_one_h, to_one), (to_two_h, to_two), (to_skip_h, to_skip), (to_out_h, to_out))
    ):
        tables.append(pltpu.make_async_copy(src, dst, small.at[n]))
        tables[n].start()
    copies = []
    for n, (src, dst) in enumerate(((w_one, w_one_v), (w_two, w_two_v))):
        for step in range(3):
            tap = 2 - step if n == 0 else step
            copy = pltpu.make_async_copy(
                src.at[pl.ds(tap * TAPS, TAPS)], dst.at[pl.ds(tap * TAPS, TAPS)], sems.at[n, tap]
            )
            copy.start()
            copies.append(copy)
    row0, col0, high, count, section = info[0], info[1], (2 + 2 * info[2]) * TS - 3, info[3], info[4]
    wide, first = info[5], 2 * section - 2
    b_in, gain_one, b_one, gain_two, b_two = [vectors[n : n + 1, :] for n in range(5)]

    lane = lax.broadcasted_iota(jnp.int32, (SPAN * EXT, EXT * ZC), 1)
    line = lax.broadcasted_iota(jnp.int32, (SPAN * EXT, EXT * ZC), 0)
    own = here[0].astype(F32) + far[1].astype(F32)
    other = (across[0].astype(F32) + far[0].astype(F32)) * section.astype(F32)
    cells = jnp.concatenate([other, own], axis=0) * inside(
        row0 - 3 + (line & (EXT - 1)), col0 - 3 + lane // ZC, high, wide
    )
    rolled = [
        cells,
        pltpu.roll(pltpu.roll(cells, SPAN * EXT - 1, 0), 3 * ZC, 1),
        pltpu.roll(pltpu.roll(cells, SPAN * EXT - 2, 0), 6 * ZC, 1),
    ]
    for x in range(STEM):
        at = [pltpu.roll(r, (EXT * ZC - ZC * x) % (EXT * ZC), 1) if x else r for r in rolled]
        packed = jnp.where(lane < 3 * ZC, at[0], jnp.where(lane < 6 * ZC, at[1], at[2]))
        lhs[:, x] = packed.astype(BF16).reshape(SPAN, EXT, EXT * ZC)

    for table in tables:
        table.wait()
    pos = lax.broadcasted_iota(jnp.int32, (STEM_ROWS, 1), 0)
    mask_one = inside(row0 - 2 + (pos & (EXT - 1)), col0 - 2 + (pos >> 4), high, wide)
    for f in range(SPAN):
        stem = b_in
        for dt in range(3):
            if f + dt - 2 >= 0:
                left = lhs[f + dt - 2].reshape(STEM_ROWS, EXT * ZC)[:, : 9 * ZC]
                stem = stem + dot(left, w_in[pl.ds(dt * 9 * ZC, 9 * ZC), :])
        act = activate(stem, gain_one) * mask_one
        if f < 2:
            act = act * (first + f >= 0).astype(F32)
        moved = dot(to_one[...], act.astype(BF16))
        act_one[f] = moved.astype(BF16).reshape(5, 5, 16, CH)
        if f >= 2:
            coarse = stem.astype(BF16)
            fine = (stem - coarse.astype(F32)).astype(BF16)
            skip[f - 2] = dot(to_skip[...], coarse) + dot(to_skip[...], fine) + b_two

    for step in range(3):
        dt = 2 - step
        copies[step].wait()
        frames = 2 + dt
        left = jnp.concatenate(
            [
                act_one[0:frames, dy : dy + 3, dx : dx + 3].reshape(frames * MID_ROWS, CH)
                for dy in range(3)
                for dx in range(3)
            ],
            axis=-1,
        )
        part = dot(left, w_one_v[pl.ds(dt * TAPS, TAPS), :])
        rows = pl.ds((SPAN - frames) * MID_ROWS, frames * MID_ROWS)
        if step == 0:
            middle[...] = part
        else:
            middle[rows, :] += part
    spot = lax.broadcasted_iota(jnp.int32, (MID_ROWS, 1), 0)
    block = spot >> 4
    block_y = (block >= 3).astype(jnp.int32) + (block >= 6).astype(jnp.int32)
    mid_y = 3 * ((spot >> 2) & 3) + block_y
    mid_x = 3 * (spot & 3) + block - 3 * block_y
    mask_two = inside(row0 - 1 + mid_y, col0 - 1 + mid_x, high, wide)
    for f in range(SPAN):
        act = activate(middle[pl.ds(f * MID_ROWS, MID_ROWS), :] + b_one, gain_two) * mask_two
        if f < 2:
            act = act * (first + f >= 0).astype(F32)
        act_two[f] = dot(to_two[...], act.astype(BF16)).astype(BF16).reshape(4, 4, 32, CH)

    total = skip[...].reshape(2 * 128, CH)
    for dt in range(3):
        copies[3 + dt].wait()
        left = jnp.concatenate(
            [
                act_two[dt : dt + 2, dy : dy + 2, dx : dx + 2].reshape(2 * 128, CH)
                for dy in range(3)
                for dx in range(3)
            ],
            axis=-1,
        )
        total = total + dot(left, w_two_v[pl.ds(dt * TAPS, TAPS), :])
    for f in range(2):
        live = first + 2 + f < count
        final = jnp.where(live, total[f * 128 : (f + 1) * 128], 0.0).astype(BF16)
        out[f] = dot(to_out[...], final)[: TS * TS].astype(BF16)


def decode(info, here, across, far, vectors, w_in, w_one, w_two):
    vmem = pl.BlockSpec(memory_space=pltpu.VMEM)
    hbm = pl.BlockSpec(memory_space=pl.ANY)
    tables = [w_in, *gathers()]
    return pl.pallas_call(
        decode_kernel,
        out_shape=jax.ShapeDtypeStruct((2, TS * TS, CH), BF16),
        in_specs=[pl.BlockSpec(memory_space=pltpu.SMEM)] + [vmem] * 4 + [hbm] * 7,
        out_specs=vmem,
        scratch_shapes=[pltpu.VMEM(t.shape, BF16) for t in tables]
        + [
            pltpu.VMEM((SPAN, STEM, EXT, EXT * ZC), BF16),
            pltpu.VMEM((SPAN, 5, 5, 16, CH), BF16),
            pltpu.VMEM((SPAN, 4, 4, 32, CH), BF16),
            pltpu.VMEM((2, 128, CH), F32),
            pltpu.VMEM((SPAN * MID_ROWS, CH), F32),
            pltpu.VMEM((3 * TAPS, CH), BF16),
            pltpu.VMEM((3 * TAPS, CH), BF16),
            pltpu.SemaphoreType.DMA((5,)),
            pltpu.SemaphoreType.DMA((2, 3)),
        ],
        compiler_params=pltpu.CompilerParams(vmem_limit_bytes=48 << 20),
        cost_estimate=pl.CostEstimate(
            flops=2 * 27 * CH * CH * (SPAN * MID_ROWS + 200), bytes_accessed=16 << 20, transcendentals=0
        ),
    )(info, here, across, far, vectors, *tables, w_one, w_two)


def slot_info(resolution, frame_counts, tile_rows, tile_cols, decoder_list, mine):
    match = decoder_list == mine
    wide = lambda t: jnp.broadcast_to(t[:, None], match.shape)
    tables = jnp.stack([tile_rows, tile_cols, wide(resolution), wide(frame_counts)])
    picked = jnp.sum(jnp.where(match[None], tables, 0), axis=(1, 2))
    place = jnp.array([0, lax.axis_size("tile") // 4 * TS - 4], jnp.int32)
    place = place + jnp.array([1, 0], jnp.int32) * lax.axis_index("section")
    return jnp.concatenate([picked, place]).astype(jnp.int32)


def local(
    latent, resolution, frame_counts, tile_rows, tile_cols, decoder_list,
    w_in, b_in, gain_one, w_one, b_one, gain_two, w_two, b_two,
):
    tiles = lax.axis_size("tile")
    video, tile = lax.axis_index("video"), lax.axis_index("tile")
    mine = video * tiles + tile
    flip = lambda a, by, count=tiles: lax.ppermute(a, "tile", [(i, i ^ by) for i in range(count)])
    unit = (2 * EXT, EXT * ZC)

    first = flip(latent, 1)
    have = jnp.concatenate([latent, first]).astype(BF16).reshape(4, *unit)
    have = jnp.concatenate([have, flip(have, 2)])
    have = jnp.concatenate([have, flip(have, 6)])
    hops = np.array([far ^ near ^ core for far in (0, 6) for near in (0, 2) for core in (0, 1)], np.int32)
    slots = (tile ^ hops)[:, None] == jnp.arange(tiles, dtype=jnp.int32)
    names = lax.dynamic_slice(decoder_list, (2 * video, 0), (2, tiles))
    names = jnp.sum(jnp.where(slots[:, None], names[None], 0), axis=-1).reshape(16)

    rows = np.array([row ^ group for row in (0, 24, 8, 16) for group in (0, tiles)], np.int32)
    match = (mine ^ rows)[:, None] == names[None, :]
    kept = jnp.sum(
        jnp.where(match[:, :, None, None], have[None], jnp.zeros((), BF16)), axis=1, dtype=F32
    ).astype(BF16)
    kept = kept[:4] + flip(kept[4:], 8, 16)
    here = kept[:2] + flip(kept[2:], 24, 16)
    across = lax.ppermute(here, "section", [(0, 1), (1, 0)])
    outward = jnp.stack([here[1], across[1]])
    far = lax.ppermute(outward, ("video", "section"), [(z, z ^ 3) for z in range(4)])

    info = slot_info(resolution, frame_counts, tile_rows, tile_cols, decoder_list, mine)
    vectors = jnp.stack([b_in, gain_one, b_one, gain_two, b_two])
    return decode(info, here, across, far, vectors, w_in, w_one, w_two)[None, None]


def solution(mesh):
    return jax.shard_map(
        local,
        mesh=mesh,
        in_specs=(P("video", "tile", "section", None, None),) + (P(),) * 13,
        out_specs=P("video", "tile", "section", None, None),
        check_vma=False,
    )
```

```python
import jax
import jax.numpy as jnp
import numpy as np
from jax import lax
from jax.experimental import pallas as pl
from jax.experimental.pallas import tpu as pltpu
from jax.sharding import PartitionSpec as P

F32 = jnp.float32
BF16 = jnp.bfloat16
ZC = 16
CH = 384
EXT = 16
TS = 10
SPAN = 4
STEM = EXT - 2
MID = EXT - 4
STEM_ROWS = STEM * EXT
MID_ROWS = MID * MID
TAPS = 9 * CH


def gathers():
    one = np.zeros((25 * 16, STEM_ROWS), np.float32)
    for ry in range(5):
        for rx in range(5):
            for j in range(16):
                y, x = 3 * (j // 4) + ry, 3 * (j % 4) + rx
                one[(ry * 5 + rx) * 16 + j, x * EXT + y] = 1
    two = np.zeros((16 * 32, MID_ROWS), np.float32)
    for ry in range(4):
        for rx in range(4):
            for j in range(25):
                y, x = 2 * (j // 5) + ry, 2 * (j % 5) + rx
                two[(ry * 4 + rx) * 32 + j, ((y % 3) * 3 + x % 3) * 16 + (y // 3) * 4 + x // 3] = 1
    skip = np.zeros((4 * 32, STEM_ROWS), np.float32)
    out = np.zeros((112, 4 * 32), np.float32)
    for y in range(TS):
        for x in range(TS):
            row = ((y % 2) * 2 + x % 2) * 32 + (y // 2) * 5 + x // 2
            skip[row, (x + 2) * EXT + y + 2] = 1
            out[y * TS + x, row] = 1
    return [jnp.asarray(a, BF16) for a in (one, two, skip, out)]


def dot(a, b):
    return jnp.dot(a, b, preferred_element_type=F32)


def activate(u, gain):
    half = 0.5 * (u * lax.rsqrt(jnp.mean(u * u, axis=-1, keepdims=True) + 1e-06) * gain)
    return half + half * jnp.tanh(half)


def inside(row, col, high, wide):
    return ((row >= 0) & (row < high) & (col >= 0) & (col < wide)).astype(F32)


def decode_kernel(
    info, here, across, far, b_in, gain_one, b_one, gain_two, b_two, w_in_h, to_one_h, to_two_h, to_skip_h, to_out_h, w_one, w_two, out,
    w_in, to_one, to_two, to_skip, to_out, lhs, act_one, act_two, skip, middle, w_one_v, w_two_v, small, sems,
):
    tables = []
    for n, (src, dst) in enumerate(
        ((w_in_h, w_in), (to_one_h, to_one), (to_two_h, to_two), (to_skip_h, to_skip), (to_out_h, to_out))
    ):
        tables.append(pltpu.make_async_copy(src, dst, small.at[n]))
        tables[n].start()
    copies = []
    for n, (src, dst) in enumerate(((w_one, w_one_v), (w_two, w_two_v))):
        for step in range(3):
            tap = 2 - step if n == 0 else step
            copy = pltpu.make_async_copy(
                src.at[pl.ds(tap * TAPS, TAPS)], dst.at[pl.ds(tap * TAPS, TAPS)], sems.at[n, tap]
            )
            copy.start()
            copies.append(copy)
    row0, col0, high, count, section = info[0], info[1], (2 + 2 * info[2]) * TS - 3, info[3], info[4]
    wide, first = info[5], 2 * section - 2
    b_in, gain_one, b_one, gain_two, b_two = [
        v[...].reshape(1, CH) for v in (b_in, gain_one, b_one, gain_two, b_two)
    ]

    lane = lax.broadcasted_iota(jnp.int32, (SPAN * EXT, EXT * ZC), 1)
    line = lax.broadcasted_iota(jnp.int32, (SPAN * EXT, EXT * ZC), 0)
    own = here[0].astype(F32) + far[1].astype(F32)
    other = (across[0].astype(F32) + far[0].astype(F32)) * section.astype(F32)
    cells = jnp.concatenate([other, own], axis=0) * inside(
        row0 - 3 + (line & (EXT - 1)), col0 - 3 + lane // ZC, high, wide
    )
    rolled = [
        cells,
        pltpu.roll(pltpu.roll(cells, SPAN * EXT - 1, 0), 3 * ZC, 1),
        pltpu.roll(pltpu.roll(cells, SPAN * EXT - 2, 0), 6 * ZC, 1),
    ]
    for x in range(STEM):
        at = [pltpu.roll(r, (EXT * ZC - ZC * x) % (EXT * ZC), 1) if x else r for r in rolled]
        packed = jnp.where(lane < 3 * ZC, at[0], jnp.where(lane < 6 * ZC, at[1], at[2]))
        lhs[:, x] = packed.astype(BF16).reshape(SPAN, EXT, EXT * ZC)

    for table in tables:
        table.wait()
    pos = lax.broadcasted_iota(jnp.int32, (STEM_ROWS, 1), 0)
    mask_one = inside(row0 - 2 + (pos & (EXT - 1)), col0 - 2 + (pos >> 4), high, wide)
    for f in range(SPAN):
        stem = b_in
        for dt in range(3):
            if f + dt - 2 >= 0:
                left = lhs[f + dt - 2].reshape(STEM_ROWS, EXT * ZC)[:, : 9 * ZC]
                stem = stem + dot(left, w_in[pl.ds(dt * 9 * ZC, 9 * ZC), :])
        act = activate(stem, gain_one) * mask_one
        if f < 2:
            act = act * (first + f >= 0).astype(F32)
        moved = dot(to_one[...], act.astype(BF16))
        act_one[f] = moved.astype(BF16).reshape(5, 5, 16, CH)
        if f >= 2:
            coarse = stem.astype(BF16)
            fine = (stem - coarse.astype(F32)).astype(BF16)
            skip[f - 2] = dot(to_skip[...], coarse) + dot(to_skip[...], fine) + b_two

    for step in range(3):
        dt = 2 - step
        copies[step].wait()
        frames = 2 + dt
        left = jnp.concatenate(
            [
                act_one[0:frames, dy : dy + 3, dx : dx + 3].reshape(frames * MID_ROWS, CH)
                for dy in range(3)
                for dx in range(3)
            ],
            axis=-1,
        )
        part = dot(left, w_one_v[pl.ds(dt * TAPS, TAPS), :])
        rows = pl.ds((SPAN - frames) * MID_ROWS, frames * MID_ROWS)
        if step == 0:
            middle[...] = part
        else:
            middle[rows, :] += part
    spot = lax.broadcasted_iota(jnp.int32, (MID_ROWS, 1), 0)
    block = spot >> 4
    block_y = (block >= 3).astype(jnp.int32) + (block >= 6).astype(jnp.int32)
    mid_y = 3 * ((spot >> 2) & 3) + block_y
    mid_x = 3 * (spot & 3) + block - 3 * block_y
    mask_two = inside(row0 - 1 + mid_y, col0 - 1 + mid_x, high, wide)
    for f in range(SPAN):
        act = activate(middle[pl.ds(f * MID_ROWS, MID_ROWS), :] + b_one, gain_two) * mask_two
        if f < 2:
            act = act * (first + f >= 0).astype(F32)
        act_two[f] = dot(to_two[...], act.astype(BF16)).astype(BF16).reshape(4, 4, 32, CH)

    total = skip[...].reshape(2 * 128, CH)
    for dt in range(3):
        copies[3 + dt].wait()
        left = jnp.concatenate(
            [
                act_two[dt : dt + 2, dy : dy + 2, dx : dx + 2].reshape(2 * 128, CH)
                for dy in range(3)
                for dx in range(3)
            ],
            axis=-1,
        )
        total = total + dot(left, w_two_v[pl.ds(dt * TAPS, TAPS), :])
    for f in range(2):
        live = first + 2 + f < count
        final = jnp.where(live, total[f * 128 : (f + 1) * 128], 0.0).astype(BF16)
        out[f] = dot(to_out[...], final)[: TS * TS].astype(BF16)


def decode(info, here, across, far, vectors, w_in, w_one, w_two):
    vmem = pl.BlockSpec(memory_space=pltpu.VMEM)
    hbm = pl.BlockSpec(memory_space=pl.ANY)
    tables = [w_in, *gathers()]
    return pl.pallas_call(
        decode_kernel,
        out_shape=jax.ShapeDtypeStruct((2, TS * TS, CH), BF16),
        in_specs=[pl.BlockSpec(memory_space=pltpu.SMEM)] + [vmem] * 8 + [hbm] * 7,
        out_specs=vmem,
        scratch_shapes=[pltpu.VMEM(t.shape, BF16) for t in tables]
        + [
            pltpu.VMEM((SPAN, STEM, EXT, EXT * ZC), BF16),
            pltpu.VMEM((SPAN, 5, 5, 16, CH), BF16),
            pltpu.VMEM((SPAN, 4, 4, 32, CH), BF16),
            pltpu.VMEM((2, 128, CH), F32),
            pltpu.VMEM((SPAN * MID_ROWS, CH), F32),
            pltpu.VMEM((3 * TAPS, CH), BF16),
            pltpu.VMEM((3 * TAPS, CH), BF16),
            pltpu.SemaphoreType.DMA((5,)),
            pltpu.SemaphoreType.DMA((2, 3)),
        ],
        compiler_params=pltpu.CompilerParams(vmem_limit_bytes=48 << 20),
        cost_estimate=pl.CostEstimate(
            flops=2 * 27 * CH * CH * (SPAN * MID_ROWS + 200), bytes_accessed=16 << 20, transcendentals=0
        ),
    )(info, here, across, far, *vectors, *tables, w_one, w_two)


def iota(shape, dim):
    return lax.broadcasted_iota(jnp.int32, shape, dim)


def slot_info(resolution, frame_counts, tile_rows, tile_cols, decoder_list, mine, width):
    shape = (6,) + decoder_list.shape
    which = iota(shape, 0)
    table = jnp.where(
        which == 0,
        tile_rows[None],
        jnp.where(
            which == 1,
            tile_cols[None],
            jnp.where(which == 2, resolution[None, :, None], frame_counts[None, :, None]),
        ),
    )
    picked = jnp.sum(jnp.where((decoder_list == mine)[None] & (which < 4), table, 0), axis=(1, 2))
    place = iota((6,), 0)
    return picked + jnp.where(place == 4, lax.axis_index("section"), jnp.where(place == 5, width, 0))


def local(
    latent, resolution, frame_counts, tile_rows, tile_cols, decoder_list,
    w_in, b_in, gain_one, w_one, b_one, gain_two, w_two, b_two,
):
    tiles = lax.axis_size("tile")
    video, tile = lax.axis_index("video"), lax.axis_index("tile")
    mine = video * tiles + tile
    flip = lambda a, by: lax.ppermute(a, "tile", [(i, i ^ by) for i in range(tiles)])
    unit = (2 * EXT, EXT * ZC)
    after = lambda done, *args: lax.optimization_barrier((done, *args))

    live = (tile < tiles // 2).astype(F32)
    first = flip(latent, 2) * live
    have = jnp.concatenate([latent.astype(BF16), first.astype(BF16)]).reshape(4, *unit)
    have = jnp.concatenate([have, flip(have, 6)])
    have = jnp.concatenate([have, flip(have, 1)])

    shape = (8, 2) + decoder_list.shape
    step = iota(shape, 0)
    hop = (step >> 2) ^ ((step >> 1) & 1) * 6 ^ (step & 1) * 2
    here = (iota(shape, 2) == 2 * video + iota(shape, 1)) & (iota(shape, 3) == tile ^ hop)
    names = jnp.sum(jnp.where(here, decoder_list, 0), axis=(2, 3))

    shape = (8, 8, 2)
    row = iota(shape, 0)
    goal = mine ^ (row & 1) * tiles ^ ((row >> 1) & 1) * 24 ^ (row >> 2) * 8
    match = (goal == names[None]).reshape(8, 16)
    kept = jnp.sum(
        jnp.where(match[:, :, None, None], have[None], jnp.zeros((), BF16)), axis=1, dtype=F32
    ).astype(BF16)
    kept = kept[:4] + flip(kept[4:], 8)
    here = kept[:2] + flip(kept[2:], 24)
    across = lax.ppermute(here, "section", [(0, 1), (1, 0)])
    outward = jnp.stack([here[1], across[1]])
    far = lax.ppermute(outward, ("video", "section"), [(z, z ^ 3) for z in range(4)])

    _, resolution, frame_counts = after(kept, resolution, frame_counts)
    info = slot_info(
        resolution, frame_counts, tile_rows, tile_cols, decoder_list, mine, tiles // 4 * TS - 4
    )
    vectors = [b_in, gain_one, b_one, gain_two, b_two]
    return decode(info, here, across, far, vectors, w_in, w_one, w_two)[None, None]


def solution(mesh):
    return jax.shard_map(
        local,
        mesh=mesh,
        in_specs=(P("video", "tile", "section", None, None),) + (P(),) * 13,
        out_specs=P("video", "tile", "section", None, None),
        check_vma=False,
    )
```

```python
import jax
import jax.numpy as jnp
import numpy as np
from jax import lax
from jax.experimental import pallas as pl
from jax.experimental.pallas import tpu as pltpu
from jax.sharding import PartitionSpec as P

F32 = jnp.float32
BF16 = jnp.bfloat16
ZC = 16
CH = 384
EXT = 16
TS = 10
SPAN = 4
STEM = EXT - 2
MID = EXT - 4
STEM_ROWS = STEM * EXT
MID_ROWS = MID * MID
TAPS = 9 * CH


def gathers():
    one = np.zeros((25 * 16, STEM_ROWS), np.float32)
    for ry in range(5):
        for rx in range(5):
            for j in range(16):
                y, x = 3 * (j // 4) + ry, 3 * (j % 4) + rx
                one[(ry * 5 + rx) * 16 + j, x * EXT + y] = 1
    two = np.zeros((16 * 32, MID_ROWS), np.float32)
    for ry in range(4):
        for rx in range(4):
            for j in range(25):
                y, x = 2 * (j // 5) + ry, 2 * (j % 5) + rx
                two[(ry * 4 + rx) * 32 + j, ((y % 3) * 3 + x % 3) * 16 + (y // 3) * 4 + x // 3] = 1
    skip = np.zeros((4 * 32, STEM_ROWS), np.float32)
    out = np.zeros((112, 4 * 32), np.float32)
    for y in range(TS):
        for x in range(TS):
            row = ((y % 2) * 2 + x % 2) * 32 + (y // 2) * 5 + x // 2
            skip[row, (x + 2) * EXT + y + 2] = 1
            out[y * TS + x, row] = 1
    return [jnp.asarray(a, BF16) for a in (one, two, skip, out)]


def dot(a, b):
    return jnp.dot(a, b, preferred_element_type=F32)


def activate(u, gain):
    half = 0.5 * (u * lax.rsqrt(jnp.mean(u * u, axis=-1, keepdims=True) + 1e-06) * gain)
    return half + half * jnp.tanh(half)


def inside(row, col, high, wide):
    return ((row >= 0) & (row < high) & (col >= 0) & (col < wide)).astype(F32)


def decode_kernel(
    info, here, across, far, b_in, gain_one, b_one, gain_two, b_two, w_in_h, to_one_h, to_two_h, to_skip_h, to_out_h, w_one, w_two, out,
    w_in, to_one, to_two, to_skip, to_out, lhs, act_one, act_two, skip, middle, w_one_v, w_two_v, small, sems,
):
    tables = []
    for n, (src, dst) in enumerate(
        ((w_in_h, w_in), (to_one_h, to_one), (to_two_h, to_two), (to_skip_h, to_skip), (to_out_h, to_out))
    ):
        tables.append(pltpu.make_async_copy(src, dst, small.at[n]))
        tables[n].start()
    copies = []
    for n, (src, dst) in enumerate(((w_one, w_one_v), (w_two, w_two_v))):
        for step in range(3):
            tap = 2 - step if n == 0 else step
            copy = pltpu.make_async_copy(
                src.at[pl.ds(tap * TAPS, TAPS)], dst.at[pl.ds(tap * TAPS, TAPS)], sems.at[n, tap]
            )
            copy.start()
            copies.append(copy)
    row0, col0, high, count, section = info[0], info[1], (2 + 2 * info[2]) * TS - 3, info[3], info[4]
    wide, first = info[5], 2 * section - 2
    b_in, gain_one, b_one, gain_two, b_two = [
        v[...].reshape(1, CH) for v in (b_in, gain_one, b_one, gain_two, b_two)
    ]

    lane = lax.broadcasted_iota(jnp.int32, (SPAN * EXT, EXT * ZC), 1)
    line = lax.broadcasted_iota(jnp.int32, (SPAN * EXT, EXT * ZC), 0)
    own = here[0].astype(F32) + far[1].astype(F32)
    other = (across[0].astype(F32) + far[0].astype(F32)) * section.astype(F32)
    cells = jnp.concatenate([other, own], axis=0) * inside(
        row0 - 3 + (line & (EXT - 1)), col0 - 3 + lane // ZC, high, wide
    )
    rolled = [
        cells,
        pltpu.roll(pltpu.roll(cells, SPAN * EXT - 1, 0), 3 * ZC, 1),
        pltpu.roll(pltpu.roll(cells, SPAN * EXT - 2, 0), 6 * ZC, 1),
    ]
    for x in range(STEM):
        at = [pltpu.roll(r, (EXT * ZC - ZC * x) % (EXT * ZC), 1) if x else r for r in rolled]
        packed = jnp.where(lane < 3 * ZC, at[0], jnp.where(lane < 6 * ZC, at[1], at[2]))
        lhs[:, x] = packed.astype(BF16).reshape(SPAN, EXT, EXT * ZC)

    for table in tables:
        table.wait()
    pos = lax.broadcasted_iota(jnp.int32, (STEM_ROWS, 1), 0)
    mask_one = inside(row0 - 2 + (pos & (EXT - 1)), col0 - 2 + (pos >> 4), high, wide)
    rows = lhs[...].reshape(SPAN * STEM_ROWS, EXT * ZC)[:, : 9 * ZC]
    part = [
        dot(rows[: (2 + dt) * STEM_ROWS], w_in[pl.ds(dt * 9 * ZC, 9 * ZC), :]) for dt in range(3)
    ]
    acts, skips = [], []
    for f in range(SPAN):
        stem = b_in
        for dt in range(3):
            if f + dt - 2 >= 0:
                at = (f + dt - 2) * STEM_ROWS
                stem = stem + part[dt][at : at + STEM_ROWS]
        act = activate(stem, gain_one) * mask_one
        if f < 2:
            act = act * (first + f >= 0).astype(F32)
        else:
            coarse = stem.astype(BF16)
            fine = (stem - coarse.astype(F32)).astype(BF16)
            skips.append(jnp.concatenate([coarse, fine], axis=0))
        acts.append(act.astype(BF16))
    moved = dot(to_one[...], jnp.concatenate(acts, axis=1)).astype(BF16)
    for f in range(SPAN):
        act_one[f] = moved[:, f * CH : (f + 1) * CH].reshape(5, 5, 16, CH)
    twice = jnp.concatenate([to_skip[...], to_skip[...]], axis=1)
    moved = dot(twice, jnp.concatenate(skips, axis=1))
    for f in range(2):
        skip[f] = moved[:, f * CH : (f + 1) * CH] + b_two

    for step in range(3):
        dt = 2 - step
        copies[step].wait()
        frames = 2 + dt
        left = jnp.concatenate(
            [
                act_one[0:frames, dy : dy + 3, dx : dx + 3].reshape(frames * MID_ROWS, CH)
                for dy in range(3)
                for dx in range(3)
            ],
            axis=-1,
        )
        part = dot(left, w_one_v[pl.ds(dt * TAPS, TAPS), :])
        rows = pl.ds((SPAN - frames) * MID_ROWS, frames * MID_ROWS)
        if step == 0:
            middle[...] = part
        else:
            middle[rows, :] += part
    spot = lax.broadcasted_iota(jnp.int32, (MID_ROWS, 1), 0)
    block = spot >> 4
    block_y = (block >= 3).astype(jnp.int32) + (block >= 6).astype(jnp.int32)
    mid_y = 3 * ((spot >> 2) & 3) + block_y
    mid_x = 3 * (spot & 3) + block - 3 * block_y
    mask_two = inside(row0 - 1 + mid_y, col0 - 1 + mid_x, high, wide)
    for f in range(SPAN):
        act = activate(middle[pl.ds(f * MID_ROWS, MID_ROWS), :] + b_one, gain_two) * mask_two
        if f < 2:
            act = act * (first + f >= 0).astype(F32)
        act_two[f] = dot(to_two[...], act.astype(BF16)).astype(BF16).reshape(4, 4, 32, CH)

    total = skip[...].reshape(2 * 128, CH)
    for dt in range(3):
        copies[3 + dt].wait()
        left = jnp.concatenate(
            [
                act_two[dt : dt + 2, dy : dy + 2, dx : dx + 2].reshape(2 * 128, CH)
                for dy in range(3)
                for dx in range(3)
            ],
            axis=-1,
        )
        total = total + dot(left, w_two_v[pl.ds(dt * TAPS, TAPS), :])
    for f in range(2):
        live = first + 2 + f < count
        final = jnp.where(live, total[f * 128 : (f + 1) * 128], 0.0).astype(BF16)
        out[f] = dot(to_out[...], final)[: TS * TS].astype(BF16)


def decode(info, here, across, far, vectors, w_in, w_one, w_two):
    vmem = pl.BlockSpec(memory_space=pltpu.VMEM)
    hbm = pl.BlockSpec(memory_space=pl.ANY)
    tables = [w_in, *gathers()]
    return pl.pallas_call(
        decode_kernel,
        out_shape=jax.ShapeDtypeStruct((2, TS * TS, CH), BF16),
        in_specs=[pl.BlockSpec(memory_space=pltpu.SMEM)] + [vmem] * 8 + [hbm] * 7,
        out_specs=vmem,
        scratch_shapes=[pltpu.VMEM(t.shape, BF16) for t in tables]
        + [
            pltpu.VMEM((SPAN, STEM, EXT, EXT * ZC), BF16),
            pltpu.VMEM((SPAN, 5, 5, 16, CH), BF16),
            pltpu.VMEM((SPAN, 4, 4, 32, CH), BF16),
            pltpu.VMEM((2, 128, CH), F32),
            pltpu.VMEM((SPAN * MID_ROWS, CH), F32),
            pltpu.VMEM((3 * TAPS, CH), BF16),
            pltpu.VMEM((3 * TAPS, CH), BF16),
            pltpu.SemaphoreType.DMA((5,)),
            pltpu.SemaphoreType.DMA((2, 3)),
        ],
        compiler_params=pltpu.CompilerParams(vmem_limit_bytes=48 << 20),
        cost_estimate=pl.CostEstimate(
            flops=2 * 27 * CH * CH * (SPAN * MID_ROWS + 200), bytes_accessed=16 << 20, transcendentals=0
        ),
    )(info, here, across, far, *vectors, *tables, w_one, w_two)


def iota(shape, dim):
    return lax.broadcasted_iota(jnp.int32, shape, dim)


def slot_info(resolution, frame_counts, tile_rows, tile_cols, decoder_list, mine, width):
    shape = (6,) + decoder_list.shape
    which = iota(shape, 0)
    table = jnp.where(
        which == 0,
        tile_rows[None],
        jnp.where(
            which == 1,
            tile_cols[None],
            jnp.where(which == 2, resolution[None, :, None], frame_counts[None, :, None]),
        ),
    )
    picked = jnp.sum(jnp.where((decoder_list == mine)[None] & (which < 4), table, 0), axis=(1, 2))
    place = iota((6,), 0)
    return picked + jnp.where(place == 4, lax.axis_index("section"), jnp.where(place == 5, width, 0))


def local(
    latent, resolution, frame_counts, tile_rows, tile_cols, decoder_list,
    w_in, b_in, gain_one, w_one, b_one, gain_two, w_two, b_two,
):
    tiles = lax.axis_size("tile")
    video, tile = lax.axis_index("video"), lax.axis_index("tile")
    mine = video * tiles + tile
    flip = lambda a, by: lax.ppermute(a, "tile", [(i, i ^ by) for i in range(tiles)])
    unit = (2 * EXT, EXT * ZC)
    after = lambda done, *args: lax.optimization_barrier((done, *args))

    live = (tile < tiles // 2).astype(F32)
    first = flip(latent, 2) * live
    have = jnp.concatenate([latent.astype(BF16), first.astype(BF16)]).reshape(4, *unit)
    have, named_by = after(have, decoder_list)
    have = jnp.concatenate([have, flip(have, 6)])
    have = jnp.concatenate([have, flip(have, 1)])

    shape = (8, 2) + decoder_list.shape
    step = iota(shape, 0)
    hop = (step >> 2) ^ ((step >> 1) & 1) * 6 ^ (step & 1) * 2
    here = (iota(shape, 2) == 2 * video + iota(shape, 1)) & (iota(shape, 3) == tile ^ hop)
    names = jnp.sum(jnp.where(here, named_by, 0), axis=(2, 3))

    shape = (8, 8, 2)
    row = iota(shape, 0)
    goal = mine ^ (row & 1) * tiles ^ ((row >> 1) & 1) * 24 ^ (row >> 2) * 8
    match = (goal == names[None]).reshape(8, 16)
    kept = jnp.sum(
        jnp.where(match[:, :, None, None], have[None], jnp.zeros((), BF16)), axis=1, dtype=F32
    ).astype(BF16)
    kept = kept[:4] + flip(kept[4:], 8)
    here = kept[:2] + flip(kept[2:], 24)
    across = lax.ppermute(here, "section", [(0, 1), (1, 0)])
    outward = jnp.stack([here[1], across[1]])
    far = lax.ppermute(outward, ("video", "section"), [(z, z ^ 3) for z in range(4)])

    _, resolution, frame_counts = after(kept, resolution, frame_counts)
    info = slot_info(
        resolution, frame_counts, tile_rows, tile_cols, decoder_list, mine, tiles // 4 * TS - 4
    )
    vectors = [b_in, gain_one, b_one, gain_two, b_two]
    return decode(info, here, across, far, vectors, w_in, w_one, w_two)[None, None]


def solution(mesh):
    return jax.shard_map(
        local,
        mesh=mesh,
        in_specs=(P("video", "tile", "section", None, None),) + (P(),) * 13,
        out_specs=P("video", "tile", "section", None, None),
        check_vma=False,
    )
```

```python
import jax
import jax.numpy as jnp
import numpy as np
from jax import lax
from jax.experimental import pallas as pl
from jax.experimental.pallas import tpu as pltpu
from jax.sharding import PartitionSpec as P

F32 = jnp.float32
BF16 = jnp.bfloat16
ZC = 16
CH = 384
EXT = 16
TS = 10
SPAN = 4
STEM = EXT - 2
MID = EXT - 4
STEM_ROWS = STEM * EXT
MID_ROWS = MID * MID
TAPS = 9 * CH


def gathers():
    one = np.zeros((25 * 16, STEM_ROWS), np.float32)
    for ry in range(5):
        for rx in range(5):
            for j in range(16):
                y, x = 3 * (j // 4) + ry, 3 * (j % 4) + rx
                one[(ry * 5 + rx) * 16 + j, x * EXT + y] = 1
    two = np.zeros((16 * 32, MID_ROWS), np.float32)
    for ry in range(4):
        for rx in range(4):
            for j in range(25):
                y, x = 2 * (j // 5) + ry, 2 * (j % 5) + rx
                two[(ry * 4 + rx) * 32 + j, ((y % 3) * 3 + x % 3) * 16 + (y // 3) * 4 + x // 3] = 1
    skip = np.zeros((4 * 32, STEM_ROWS), np.float32)
    out = np.zeros((112, 4 * 32), np.float32)
    for y in range(TS):
        for x in range(TS):
            row = ((y % 2) * 2 + x % 2) * 32 + (y // 2) * 5 + x // 2
            skip[row, (x + 2) * EXT + y + 2] = 1
            out[y * TS + x, row] = 1
    return [jnp.asarray(a, BF16) for a in (one, two, skip, out)]


def dot(a, b):
    return jnp.dot(a, b, preferred_element_type=F32)


def activate(u, gain):
    half = 0.5 * (u * lax.rsqrt(jnp.mean(u * u, axis=-1, keepdims=True) + 1e-06) * gain)
    return half + half * jnp.tanh(half)


def inside(row, col, high, wide):
    return ((row >= 0) & (row < high) & (col >= 0) & (col < wide)).astype(F32)


def decode_kernel(
    info, here, across, far, b_in, gain_one, b_one, gain_two, b_two, w_in_h, to_one_h, to_two_h, to_skip_h, to_out_h, w_one, w_two, out,
    w_in, to_one, to_two, to_skip, to_out, lhs, act_one, act_two, skip, middle, w_one_v, w_two_v, small, sems,
):
    first_frame = 2 * info[4]

    @pl.when(first_frame < info[3])
    def _():
        tables = []
        for n, (src, dst) in enumerate(
            ((w_in_h, w_in), (to_one_h, to_one), (to_two_h, to_two), (to_skip_h, to_skip), (to_out_h, to_out))
        ):
            tables.append(pltpu.make_async_copy(src, dst, small.at[n]))
            tables[n].start()
        copies = []
        for n, (src, dst) in enumerate(((w_one, w_one_v), (w_two, w_two_v))):
            for step in range(3):
                tap = 2 - step if n == 0 else step
                copy = pltpu.make_async_copy(
                    src.at[pl.ds(tap * TAPS, TAPS)], dst.at[pl.ds(tap * TAPS, TAPS)], sems.at[n, tap]
                )
                copies.append(copy)
                if tap:
                    copy.start()
                else:
                    pl.when(info[4] == 1)(copy.start)
        row0, col0, high, count, section = info[0], info[1], (2 + 2 * info[2]) * TS - 3, info[3], info[4]
        wide, first = info[5], 2 * section - 2
        bias_in, gain_1, bias_one, gain_2, bias_two = [
            v[...].reshape(1, CH) for v in (b_in, gain_one, b_one, gain_two, b_two)
        ]

        lane = lax.broadcasted_iota(jnp.int32, (SPAN * EXT, EXT * ZC), 1)
        line = lax.broadcasted_iota(jnp.int32, (SPAN * EXT, EXT * ZC), 0)
        own = here[0].astype(F32) + far[1].astype(F32)
        other = (across[0].astype(F32) + far[0].astype(F32)) * section.astype(F32)
        cells = jnp.concatenate([other, own], axis=0) * inside(
            row0 - 3 + (line & (EXT - 1)), col0 - 3 + lane // ZC, high, wide
        )
        rolled = [
            cells,
            pltpu.roll(pltpu.roll(cells, SPAN * EXT - 1, 0), 3 * ZC, 1),
            pltpu.roll(pltpu.roll(cells, SPAN * EXT - 2, 0), 6 * ZC, 1),
        ]
        for x in range(STEM):
            at = [pltpu.roll(r, (EXT * ZC - ZC * x) % (EXT * ZC), 1) if x else r for r in rolled]
            packed = jnp.where(lane < 3 * ZC, at[0], jnp.where(lane < 6 * ZC, at[1], at[2]))
            lhs[:, x] = packed.astype(BF16).reshape(SPAN, EXT, EXT * ZC)

        for table in tables:
            table.wait()
        pos = lax.broadcasted_iota(jnp.int32, (STEM_ROWS, 1), 0)
        mask_one = inside(row0 - 2 + (pos & (EXT - 1)), col0 - 2 + (pos >> 4), high, wide)
        rows = lhs[...].reshape(SPAN * STEM_ROWS, EXT * ZC)[:, : 9 * ZC]
        part = [
            dot(rows[: (2 + dt) * STEM_ROWS], w_in[pl.ds(dt * 9 * ZC, 9 * ZC), :]) for dt in range(3)
        ]
        acts, skips = [], []
        for f in range(SPAN):
            stem = bias_in
            for dt in range(3):
                if f + dt - 2 >= 0:
                    at = (f + dt - 2) * STEM_ROWS
                    stem = stem + part[dt][at : at + STEM_ROWS]
            act = activate(stem, gain_1) * mask_one
            if f < 2:
                act = act * (first + f >= 0).astype(F32)
            else:
                coarse = stem.astype(BF16)
                fine = (stem - coarse.astype(F32)).astype(BF16)
                skips.append(jnp.concatenate([coarse, fine], axis=0))
            acts.append(act.astype(BF16))
        moved = dot(to_one[...], jnp.concatenate(acts, axis=1)).astype(BF16)
        for f in range(SPAN):
            act_one[f] = moved[:, f * CH : (f + 1) * CH].reshape(5, 5, 16, CH)
        twice = jnp.concatenate([to_skip[...], to_skip[...]], axis=1)
        moved = dot(twice, jnp.concatenate(skips, axis=1))
        for f in range(2):
            skip[f] = moved[:, f * CH : (f + 1) * CH] + bias_two

        def taps(ref, start, frames, side, rows):
            return jnp.concatenate(
                [
                    ref[start : start + frames, dy : dy + side, dx : dx + side].reshape(frames * rows, CH)
                    for dy in range(3)
                    for dx in range(3)
                ],
                axis=-1,
            )

        def add_middle(dt):
            frames = 2 + dt
            copies[2 - dt].wait()
            part = dot(taps(act_one, 0, frames, 3, MID_ROWS), w_one_v[pl.ds(dt * TAPS, TAPS), :])
            rows = pl.ds((SPAN - frames) * MID_ROWS, frames * MID_ROWS)
            if dt == 2:
                middle[rows, :] = part
            else:
                middle[rows, :] += part

        add_middle(2)
        add_middle(1)

        @pl.when(section == 1)
        def _():
            add_middle(0)

        spot = lax.broadcasted_iota(jnp.int32, (MID_ROWS, 1), 0)
        block = spot >> 4
        block_y = (block >= 3).astype(jnp.int32) + (block >= 6).astype(jnp.int32)
        mid_y = 3 * ((spot >> 2) & 3) + block_y
        mid_x = 3 * (spot & 3) + block - 3 * block_y
        mask_two = inside(row0 - 1 + mid_y, col0 - 1 + mid_x, high, wide)
        for f in range(SPAN):
            act = activate(middle[pl.ds(f * MID_ROWS, MID_ROWS), :] + bias_one, gain_2) * mask_two
            if f < 2:
                act = act * (first + f >= 0).astype(F32)
            act_two[f] = dot(to_two[...], act.astype(BF16)).astype(BF16).reshape(4, 4, 32, CH)

        def add_last(dt):
            copies[3 + dt].wait()
            part = dot(taps(act_two, dt, 2, 2, 128), w_two_v[pl.ds(dt * TAPS, TAPS), :])
            skip[...] += part.reshape(2, 128, CH)

        @pl.when(section == 1)
        def _():
            add_last(0)

        add_last(1)
        add_last(2)
        total = skip[...].reshape(2 * 128, CH)
        for f in range(2):
            live = first + 2 + f < count
            final = jnp.where(live, total[f * 128 : (f + 1) * 128], 0.0).astype(BF16)
            out[f] = dot(to_out[...], final)[: TS * TS].astype(BF16)

    @pl.when(first_frame >= info[3])
    def _():
        out[...] = jnp.zeros_like(out)


def decode(info, here, across, far, vectors, w_in, w_one, w_two):
    vmem = pl.BlockSpec(memory_space=pltpu.VMEM)
    hbm = pl.BlockSpec(memory_space=pl.ANY)
    tables = [w_in, *gathers()]
    return pl.pallas_call(
        decode_kernel,
        out_shape=jax.ShapeDtypeStruct((2, TS * TS, CH), BF16),
        in_specs=[pl.BlockSpec(memory_space=pltpu.SMEM)] + [vmem] * 8 + [hbm] * 7,
        out_specs=vmem,
        scratch_shapes=[pltpu.VMEM(t.shape, BF16) for t in tables]
        + [
            pltpu.VMEM((SPAN, STEM, EXT, EXT * ZC), BF16),
            pltpu.VMEM((SPAN, 5, 5, 16, CH), BF16),
            pltpu.VMEM((SPAN, 4, 4, 32, CH), BF16),
            pltpu.VMEM((2, 128, CH), F32),
            pltpu.VMEM((SPAN * MID_ROWS, CH), F32),
            pltpu.VMEM((3 * TAPS, CH), BF16),
            pltpu.VMEM((3 * TAPS, CH), BF16),
            pltpu.SemaphoreType.DMA((5,)),
            pltpu.SemaphoreType.DMA((2, 3)),
        ],
        compiler_params=pltpu.CompilerParams(vmem_limit_bytes=48 << 20),
        cost_estimate=pl.CostEstimate(
            flops=2 * 27 * CH * CH * (SPAN * MID_ROWS + 200), bytes_accessed=16 << 20, transcendentals=0
        ),
    )(info, here, across, far, *vectors, *tables, w_one, w_two)


def iota(shape, dim):
    return lax.broadcasted_iota(jnp.int32, shape, dim)


def slot_info(resolution, frame_counts, tile_rows, tile_cols, decoder_list, mine, width):
    shape = (6,) + decoder_list.shape
    which = iota(shape, 0)
    table = jnp.where(
        which == 0,
        tile_rows[None],
        jnp.where(
            which == 1,
            tile_cols[None],
            jnp.where(which == 2, resolution[None, :, None], frame_counts[None, :, None]),
        ),
    )
    picked = jnp.sum(jnp.where((decoder_list == mine)[None] & (which < 4), table, 0), axis=(1, 2))
    place = iota((6,), 0)
    return picked + jnp.where(place == 4, lax.axis_index("section"), jnp.where(place == 5, width, 0))


def local(
    latent, resolution, frame_counts, tile_rows, tile_cols, decoder_list,
    w_in, b_in, gain_one, w_one, b_one, gain_two, w_two, b_two,
):
    tiles = lax.axis_size("tile")
    video, tile = lax.axis_index("video"), lax.axis_index("tile")
    mine = video * tiles + tile
    flip = lambda a, by: lax.ppermute(a, "tile", [(i, i ^ by) for i in range(tiles)])
    unit = (2 * EXT, EXT * ZC)
    after = lambda done, *args: lax.optimization_barrier((done, *args))

    live = (tile < tiles // 2).astype(F32)
    first = flip(latent, 2) * live
    have = jnp.concatenate([latent.astype(BF16), first.astype(BF16)]).reshape(4, *unit)
    have, named_by = after(have, decoder_list)
    have = jnp.concatenate([have, flip(have, 6)])
    have = jnp.concatenate([have, flip(have, 1)])

    shape = (8, 2) + decoder_list.shape
    step = iota(shape, 0)
    hop = (step >> 2) ^ ((step >> 1) & 1) * 6 ^ (step & 1) * 2
    here = (iota(shape, 2) == 2 * video + iota(shape, 1)) & (iota(shape, 3) == tile ^ hop)
    names = jnp.sum(jnp.where(here, named_by, 0), axis=(2, 3))

    shape = (8, 8, 2)
    row = iota(shape, 0)
    goal = mine ^ (row & 1) * tiles ^ ((row >> 1) & 1) * 24 ^ (row >> 2) * 8
    match = (goal == names[None]).reshape(8, 16)
    kept = jnp.sum(
        jnp.where(match[:, :, None, None], have[None], jnp.zeros((), BF16)), axis=1, dtype=F32
    ).astype(BF16)
    kept = kept[:4] + flip(kept[4:], 8)
    here = kept[:2] + flip(kept[2:], 24)
    across = lax.ppermute(here, "section", [(0, 1), (1, 0)])
    outward = jnp.stack([here[1], across[1]])
    far = lax.ppermute(outward, ("video", "section"), [(z, z ^ 3) for z in range(4)])

    _, resolution, frame_counts = after(kept, resolution, frame_counts)
    info = slot_info(
        resolution, frame_counts, tile_rows, tile_cols, decoder_list, mine, tiles // 4 * TS - 4
    )
    vectors = [b_in, gain_one, b_one, gain_two, b_two]
    return decode(info, here, across, far, vectors, w_in, w_one, w_two)[None, None]


def solution(mesh):
    return jax.shard_map(
        local,
        mesh=mesh,
        in_specs=(P("video", "tile", "section", None, None),) + (P(),) * 13,
        out_specs=P("video", "tile", "section", None, None),
        check_vma=False,
    )
```

```python
import jax
import jax.numpy as jnp
import numpy as np
from jax import lax
from jax.experimental import pallas as pl
from jax.experimental.pallas import tpu as pltpu
from jax.sharding import PartitionSpec as P

F32 = jnp.float32
BF16 = jnp.bfloat16
ZC = 16
CH = 384
EXT = 16
TS = 10
SPAN = 4
STEM = EXT - 2
MID = EXT - 4
STEM_ROWS = STEM * EXT
MID_ROWS = MID * MID
TAPS = 9 * CH


def gathers():
    one = np.zeros((25 * 16, STEM_ROWS), np.float32)
    for ry in range(5):
        for rx in range(5):
            for j in range(16):
                y, x = 3 * (j // 4) + ry, 3 * (j % 4) + rx
                one[(ry * 5 + rx) * 16 + j, x * EXT + y] = 1
    two = np.zeros((16 * 32, MID_ROWS), np.float32)
    for ry in range(4):
        for rx in range(4):
            for j in range(25):
                y, x = 2 * (j // 5) + ry, 2 * (j % 5) + rx
                two[(ry * 4 + rx) * 32 + j, ((y % 3) * 3 + x % 3) * 16 + (y // 3) * 4 + x // 3] = 1
    skip = np.zeros((4 * 32, STEM_ROWS), np.float32)
    out = np.zeros((112, 4 * 32), np.float32)
    for y in range(TS):
        for x in range(TS):
            row = ((y % 2) * 2 + x % 2) * 32 + (y // 2) * 5 + x // 2
            skip[row, (x + 2) * EXT + y + 2] = 1
            out[y * TS + x, row] = 1
    return [jnp.asarray(a, BF16) for a in (one, two, skip, out)]


def dot(a, b):
    return jnp.dot(a, b, preferred_element_type=F32)


def activate(u, gain):
    half = 0.5 * (u * lax.rsqrt(jnp.mean(u * u, axis=-1, keepdims=True) + 1e-06) * gain)
    return half + half * jnp.tanh(half)


def inside(row, col, high, wide):
    return ((row >= 0) & (row < high) & (col >= 0) & (col < wide)).astype(F32)


def decode_kernel(
    info, here, across, far, b_in, gain_one, b_one, gain_two, b_two, w_in_h, to_one_h, to_two_h, to_skip_h, to_out_h, w_one, w_two, out,
    w_in, to_one, to_two, to_skip, to_out, lhs, act_one, act_two, skip, middle, w_one_v, w_two_v, small, sems,
):
    first_frame = 2 * info[4]

    @pl.when(first_frame < info[3])
    def _():
        tables = []
        for n, (src, dst) in enumerate(
            ((w_in_h, w_in), (to_one_h, to_one), (to_two_h, to_two), (to_skip_h, to_skip), (to_out_h, to_out))
        ):
            tables.append(pltpu.make_async_copy(src, dst, small.at[n]))
            tables[n].start()
        copies = []
        for n, (src, dst) in enumerate(((w_one, w_one_v), (w_two, w_two_v))):
            for step in range(3):
                tap = 2 - step if n == 0 else step
                copy = pltpu.make_async_copy(
                    src.at[pl.ds(tap * TAPS, TAPS)], dst.at[pl.ds(tap * TAPS, TAPS)], sems.at[n, tap]
                )
                copies.append(copy)
                if tap:
                    copy.start()
                else:
                    pl.when(info[4] == 1)(copy.start)
        row0, col0, high, count, section = info[0], info[1], (2 + 2 * info[2]) * TS - 3, info[3], info[4]
        wide, first = info[5], 2 * section - 2
        bias_in, gain_1, bias_one, gain_2, bias_two = [
            v[...].reshape(1, CH) for v in (b_in, gain_one, b_one, gain_two, b_two)
        ]

        lane = lax.broadcasted_iota(jnp.int32, (SPAN * EXT, EXT * ZC), 1)
        line = lax.broadcasted_iota(jnp.int32, (SPAN * EXT, EXT * ZC), 0)
        own = here[0].astype(F32) + far[1].astype(F32)
        other = (across[...].astype(F32) + far[0].astype(F32)) * section.astype(F32)
        cells = jnp.concatenate([other, own], axis=0) * inside(
            row0 - 3 + (line & (EXT - 1)), col0 - 3 + lane // ZC, high, wide
        )
        rolled = [
            cells,
            pltpu.roll(pltpu.roll(cells, SPAN * EXT - 1, 0), 3 * ZC, 1),
            pltpu.roll(pltpu.roll(cells, SPAN * EXT - 2, 0), 6 * ZC, 1),
        ]
        for x in range(STEM):
            at = [pltpu.roll(r, (EXT * ZC - ZC * x) % (EXT * ZC), 1) if x else r for r in rolled]
            packed = jnp.where(lane < 3 * ZC, at[0], jnp.where(lane < 6 * ZC, at[1], at[2]))
            lhs[:, x] = packed.astype(BF16).reshape(SPAN, EXT, EXT * ZC)

        for table in tables:
            table.wait()
        pos = lax.broadcasted_iota(jnp.int32, (STEM_ROWS, 1), 0)
        mask_one = inside(row0 - 2 + (pos & (EXT - 1)), col0 - 2 + (pos >> 4), high, wide)
        rows = lhs[...].reshape(SPAN * STEM_ROWS, EXT * ZC)[:, : 9 * ZC]
        part = [
            dot(rows[: (2 + dt) * STEM_ROWS], w_in[pl.ds(dt * 9 * ZC, 9 * ZC), :]) for dt in range(3)
        ]
        acts, skips = [], []
        for f in range(SPAN):
            stem = bias_in
            for dt in range(3):
                if f + dt - 2 >= 0:
                    at = (f + dt - 2) * STEM_ROWS
                    stem = stem + part[dt][at : at + STEM_ROWS]
            act = activate(stem, gain_1) * mask_one
            if f < 2:
                act = act * (first + f >= 0).astype(F32)
            else:
                coarse = stem.astype(BF16)
                fine = (stem - coarse.astype(F32)).astype(BF16)
                skips.append(jnp.concatenate([coarse, fine], axis=0))
            acts.append(act.astype(BF16))
        moved = dot(to_one[...], jnp.concatenate(acts, axis=1)).astype(BF16)
        for f in range(SPAN):
            act_one[f] = moved[:, f * CH : (f + 1) * CH].reshape(5, 5, 16, CH)
        twice = jnp.concatenate([to_skip[...], to_skip[...]], axis=1)
        moved = dot(twice, jnp.concatenate(skips, axis=1))
        for f in range(2):
            skip[f] = moved[:, f * CH : (f + 1) * CH] + bias_two

        def taps(ref, start, frames, side, rows):
            return jnp.concatenate(
                [
                    ref[start : start + frames, dy : dy + side, dx : dx + side].reshape(frames * rows, CH)
                    for dy in range(3)
                    for dx in range(3)
                ],
                axis=-1,
            )

        def add_middle(dt):
            frames = 2 + dt
            copies[2 - dt].wait()
            part = dot(taps(act_one, 0, frames, 3, MID_ROWS), w_one_v[pl.ds(dt * TAPS, TAPS), :])
            rows = pl.ds((SPAN - frames) * MID_ROWS, frames * MID_ROWS)
            if dt == 2:
                middle[rows, :] = part
            else:
                middle[rows, :] += part

        add_middle(2)
        add_middle(1)

        @pl.when(section == 1)
        def _():
            add_middle(0)

        spot = lax.broadcasted_iota(jnp.int32, (MID_ROWS, 1), 0)
        block = spot >> 4
        block_y = (block >= 3).astype(jnp.int32) + (block >= 6).astype(jnp.int32)
        mid_y = 3 * ((spot >> 2) & 3) + block_y
        mid_x = 3 * (spot & 3) + block - 3 * block_y
        mask_two = inside(row0 - 1 + mid_y, col0 - 1 + mid_x, high, wide)
        for f in range(SPAN):
            act = activate(middle[pl.ds(f * MID_ROWS, MID_ROWS), :] + bias_one, gain_2) * mask_two
            if f < 2:
                act = act * (first + f >= 0).astype(F32)
            act_two[f] = dot(to_two[...], act.astype(BF16)).astype(BF16).reshape(4, 4, 32, CH)

        def add_last(dt):
            copies[3 + dt].wait()
            part = dot(taps(act_two, dt, 2, 2, 128), w_two_v[pl.ds(dt * TAPS, TAPS), :])
            skip[...] += part.reshape(2, 128, CH)

        @pl.when(section == 1)
        def _():
            add_last(0)

        add_last(1)
        add_last(2)
        total = skip[...].reshape(2 * 128, CH)
        for f in range(2):
            live = first + 2 + f < count
            final = jnp.where(live, total[f * 128 : (f + 1) * 128], 0.0).astype(BF16)
            out[f] = dot(to_out[...], final)[: TS * TS].astype(BF16)

    @pl.when(first_frame >= info[3])
    def _():
        out[...] = jnp.zeros_like(out)


def decode(info, here, across, far, vectors, w_in, w_one, w_two):
    vmem = pl.BlockSpec(memory_space=pltpu.VMEM)
    hbm = pl.BlockSpec(memory_space=pl.ANY)
    tables = [w_in, *gathers()]
    return pl.pallas_call(
        decode_kernel,
        out_shape=jax.ShapeDtypeStruct((2, TS * TS, CH), BF16),
        in_specs=[pl.BlockSpec(memory_space=pltpu.SMEM)] + [vmem] * 8 + [hbm] * 7,
        out_specs=vmem,
        scratch_shapes=[pltpu.VMEM(t.shape, BF16) for t in tables]
        + [
            pltpu.VMEM((SPAN, STEM, EXT, EXT * ZC), BF16),
            pltpu.VMEM((SPAN, 5, 5, 16, CH), BF16),
            pltpu.VMEM((SPAN, 4, 4, 32, CH), BF16),
            pltpu.VMEM((2, 128, CH), F32),
            pltpu.VMEM((SPAN * MID_ROWS, CH), F32),
            pltpu.VMEM((3 * TAPS, CH), BF16),
            pltpu.VMEM((3 * TAPS, CH), BF16),
            pltpu.SemaphoreType.DMA((5,)),
            pltpu.SemaphoreType.DMA((2, 3)),
        ],
        compiler_params=pltpu.CompilerParams(vmem_limit_bytes=48 << 20),
        cost_estimate=pl.CostEstimate(
            flops=2 * 27 * CH * CH * (SPAN * MID_ROWS + 200), bytes_accessed=16 << 20, transcendentals=0
        ),
    )(info, here, across, far, *vectors, *tables, w_one, w_two)


def iota(shape, dim):
    return lax.broadcasted_iota(jnp.int32, shape, dim)


def slot_info(resolution, frame_counts, tile_rows, tile_cols, decoder_list, mine, width):
    shape = (6,) + decoder_list.shape
    which = iota(shape, 0)
    table = jnp.where(
        which == 0,
        tile_rows[None],
        jnp.where(
            which == 1,
            tile_cols[None],
            jnp.where(which == 2, resolution[None, :, None], frame_counts[None, :, None]),
        ),
    )
    picked = jnp.sum(jnp.where((decoder_list == mine)[None] & (which < 4), table, 0), axis=(1, 2))
    place = iota((6,), 0)
    return picked + jnp.where(place == 4, lax.axis_index("section"), jnp.where(place == 5, width, 0))


def local(
    latent, resolution, frame_counts, tile_rows, tile_cols, decoder_list,
    w_in, b_in, gain_one, w_one, b_one, gain_two, w_two, b_two,
):
    tiles = lax.axis_size("tile")
    video, tile = lax.axis_index("video"), lax.axis_index("tile")
    mine = video * tiles + tile
    flip = lambda a, by: lax.ppermute(a, "tile", [(i, i ^ by) for i in range(tiles)])
    unit = (2 * EXT, EXT * ZC)
    after = lambda done, *args: lax.optimization_barrier((done, *args))

    live = (tile < tiles // 2).astype(F32)
    got = [flip(latent, by) * live for by in (2, 6, 4)]
    have = jnp.concatenate([a.astype(BF16) for a in (latent, *got)]).reshape(8, *unit)
    have, named_by = after(have, decoder_list)
    have = jnp.concatenate([have, flip(have, 1)])

    shape = (8, 2) + decoder_list.shape
    step = iota(shape, 0)
    hop = (step >> 2) ^ ((step >> 1) & 1) * 6 ^ (step & 1) * 2
    here = (iota(shape, 2) == 2 * video + iota(shape, 1)) & (iota(shape, 3) == tile ^ hop)
    names = jnp.sum(jnp.where(here, named_by, 0), axis=(2, 3))

    shape = (8, 8, 2)
    row = iota(shape, 0)
    goal = mine ^ (row & 1) * tiles ^ ((row >> 1) & 1) * 24 ^ (row >> 2) * 8
    match = (goal == names[None]).reshape(8, 16)
    kept = jnp.sum(
        jnp.where(match[:, :, None, None], have[None], jnp.zeros((), BF16)), axis=1, dtype=F32
    ).astype(BF16)
    here = kept[:2] + flip(kept[4:6], 8) + flip(kept[2:4], 24) + flip(kept[6:], 16)
    around = lambda a, by: lax.ppermute(a, ("video", "section"), [(z, z ^ by) for z in range(4)])
    far = jnp.stack([around(here[1], 3), around(here[1], 2)])
    across = around(here[0], 1)

    _, resolution, frame_counts = after(kept, resolution, frame_counts)
    info = slot_info(
        resolution, frame_counts, tile_rows, tile_cols, decoder_list, mine, tiles // 4 * TS - 4
    )
    vectors = [b_in, gain_one, b_one, gain_two, b_two]
    return decode(info, here, across, far, vectors, w_in, w_one, w_two)[None, None]


def solution(mesh):
    return jax.shard_map(
        local,
        mesh=mesh,
        in_specs=(P("video", "tile", "section", None, None),) + (P(),) * 13,
        out_specs=P("video", "tile", "section", None, None),
        check_vma=False,
    )
```

```python
import jax
import jax.numpy as jnp
import numpy as np
from jax import lax
from jax.experimental import pallas as pl
from jax.experimental.pallas import tpu as pltpu
from jax.sharding import PartitionSpec as P

F32 = jnp.float32
BF16 = jnp.bfloat16
ZC = 16
CH = 384
EXT = 16
TS = 10
SPAN = 4
STEM = EXT - 2
MID = EXT - 4
STEM_ROWS = STEM * EXT
MID_ROWS = MID * MID
TAPS = 9 * CH


def gathers():
    one = np.zeros((25 * 16, STEM_ROWS), np.float32)
    for ry in range(5):
        for rx in range(5):
            for j in range(16):
                y, x = 3 * (j // 4) + ry, 3 * (j % 4) + rx
                one[(ry * 5 + rx) * 16 + j, x * EXT + y] = 1
    two = np.zeros((16 * 32, MID_ROWS), np.float32)
    for ry in range(4):
        for rx in range(4):
            for j in range(25):
                y, x = 2 * (j // 5) + ry, 2 * (j % 5) + rx
                two[(ry * 4 + rx) * 32 + j, ((y % 3) * 3 + x % 3) * 16 + (y // 3) * 4 + x // 3] = 1
    skip = np.zeros((4 * 32, STEM_ROWS), np.float32)
    out = np.zeros((112, 4 * 32), np.float32)
    for y in range(TS):
        for x in range(TS):
            row = ((y % 2) * 2 + x % 2) * 32 + (y // 2) * 5 + x // 2
            skip[row, (x + 2) * EXT + y + 2] = 1
            out[y * TS + x, row] = 1
    return [jnp.asarray(a, BF16) for a in (one, two, skip, out)]


def dot(a, b):
    return jnp.dot(a, b, preferred_element_type=F32)


def activate(u, gain):
    half = 0.5 * (u * lax.rsqrt(jnp.mean(u * u, axis=-1, keepdims=True) + 1e-06) * gain)
    return half + half * jnp.tanh(half)


def inside(row, col, high, wide):
    return ((row >= 0) & (row < high) & (col >= 0) & (col < wide)).astype(F32)


def decode_kernel(
    info, here, across, far, b_in, gain_one, b_one, gain_two, b_two, w_in_h, to_one_h, to_two_h, to_skip_h, to_out_h, w_one, w_two, out,
    w_in, to_one, to_two, to_skip, to_out, lhs, act_one, act_two, skip, middle, w_one_v, w_two_v, small, sems,
):
    row0, col0, high, count, section = info[0], info[1], (2 + 2 * info[2]) * TS - 3, info[3], info[4]
    wide, first = info[5], 2 * section - 2

    def taps(ref, start, frames, side, rows):
        return jnp.concatenate(
            [
                ref[start : start + frames, dy : dy + side, dx : dx + side].reshape(frames * rows, CH)
                for dy in range(3)
                for dx in range(3)
            ],
            axis=-1,
        )

    def work(low):
        known = SPAN - low
        tables = []
        for n, (src, dst) in enumerate(
            ((w_in_h, w_in), (to_one_h, to_one), (to_two_h, to_two), (to_skip_h, to_skip), (to_out_h, to_out))
        ):
            tables.append(pltpu.make_async_copy(src, dst, small.at[n]))
            tables[n].start()
        copies = {}
        for n, (src, dst) in enumerate(((w_one, w_one_v), (w_two, w_two_v))):
            for step in range(3):
                tap = 2 - step if n == 0 else step
                if tap == 0 and low:
                    continue
                copy = pltpu.make_async_copy(
                    src.at[pl.ds(tap * TAPS, TAPS)], dst.at[pl.ds(tap * TAPS, TAPS)], sems.at[n, tap]
                )
                copy.start()
                copies[n, tap] = copy
        bias_in, gain_1, bias_one, gain_2, bias_two = [
            v[...].reshape(1, CH) for v in (b_in, gain_one, b_one, gain_two, b_two)
        ]

        shape = (known * EXT, EXT * ZC)
        lane = lax.broadcasted_iota(jnp.int32, shape, 1)
        line = lax.broadcasted_iota(jnp.int32, shape, 0)
        cells = here[0].astype(F32) + far[1].astype(F32)
        if not low:
            other = across[...].astype(F32) + far[0].astype(F32)
            cells = jnp.concatenate([other, cells], axis=0)
        cells = cells * inside(row0 - 3 + (line & (EXT - 1)), col0 - 3 + lane // ZC, high, wide)
        rolled = [
            cells,
            pltpu.roll(pltpu.roll(cells, known * EXT - 1, 0), 3 * ZC, 1),
            pltpu.roll(pltpu.roll(cells, known * EXT - 2, 0), 6 * ZC, 1),
        ]
        for x in range(STEM):
            at = [pltpu.roll(r, EXT * ZC - ZC * x, 1) if x else r for r in rolled]
            packed = jnp.where(lane < 3 * ZC, at[0], jnp.where(lane < 6 * ZC, at[1], at[2]))
            lhs[low:SPAN, x] = packed.astype(BF16).reshape(known, EXT, EXT * ZC)

        for table in tables:
            table.wait()
        pos = lax.broadcasted_iota(jnp.int32, (STEM_ROWS, 1), 0)
        mask_one = inside(row0 - 2 + (pos & (EXT - 1)), col0 - 2 + (pos >> 4), high, wide)
        rows = lhs[low:SPAN].reshape(known * STEM_ROWS, EXT * ZC)[:, : 9 * ZC]
        part = {
            dt: dot(rows[: (known - 2 + dt) * STEM_ROWS], w_in[pl.ds(dt * 9 * ZC, 9 * ZC), :])
            for dt in range(3)
            if known - 2 + dt > 0
        }
        acts, skips = [], []
        for f in range(low, SPAN):
            stem = bias_in
            for dt in range(3):
                if f + dt - 2 >= low:
                    at = (f + dt - 2 - low) * STEM_ROWS
                    stem = stem + part[dt][at : at + STEM_ROWS]
            act = activate(stem, gain_1) * mask_one
            if f >= 2:
                coarse = stem.astype(BF16)
                fine = (stem - coarse.astype(F32)).astype(BF16)
                skips.append(jnp.concatenate([coarse, fine], axis=0))
            acts.append(act.astype(BF16))
        moved = dot(to_one[...], jnp.concatenate(acts, axis=1)).astype(BF16)
        for f in range(low, SPAN):
            act_one[f] = moved[:, (f - low) * CH : (f - low + 1) * CH].reshape(5, 5, 16, CH)
        twice = jnp.concatenate([to_skip[...], to_skip[...]], axis=1)
        moved = dot(twice, jnp.concatenate(skips, axis=1))
        for f in range(2):
            skip[f] = moved[:, f * CH : (f + 1) * CH] + bias_two

        for dt in (2, 1, 0):
            frames = known - 2 + dt
            if frames > 0:
                copies[0, dt].wait()
                add = dot(taps(act_one, low, frames, 3, MID_ROWS), w_one_v[pl.ds(dt * TAPS, TAPS), :])
                at = pl.ds((SPAN - frames) * MID_ROWS, frames * MID_ROWS)
                if dt == 2:
                    middle[at, :] = add
                else:
                    middle[at, :] += add
        spot = lax.broadcasted_iota(jnp.int32, (MID_ROWS, 1), 0)
        block = spot >> 4
        block_y = (block >= 3).astype(jnp.int32) + (block >= 6).astype(jnp.int32)
        mid_y = 3 * ((spot >> 2) & 3) + block_y
        mid_x = 3 * (spot & 3) + block - 3 * block_y
        mask_two = inside(row0 - 1 + mid_y, col0 - 1 + mid_x, high, wide)
        for f in range(low, SPAN):
            act = activate(middle[pl.ds(f * MID_ROWS, MID_ROWS), :] + bias_one, gain_2) * mask_two
            act_two[f] = dot(to_two[...], act.astype(BF16)).astype(BF16).reshape(4, 4, 32, CH)

        total = skip[...].reshape(2 * 128, CH)
        for dt in range(3):
            start = max(dt, low)
            if start > dt + 1:
                continue
            copies[1, dt].wait()
            frames = dt + 2 - start
            add = dot(taps(act_two, start, frames, 2, 128), w_two_v[pl.ds(dt * TAPS, TAPS), :])
            if frames == 1:
                add = jnp.concatenate([jnp.zeros((128, CH), F32), add], axis=0)
            total = total + add
        for f in range(2):
            live = first + 2 + f < count
            final = jnp.where(live, total[f * 128 : (f + 1) * 128], 0.0).astype(BF16)
            out[f] = dot(to_out[...], final)[: TS * TS].astype(BF16)

    valid = 2 * section < count
    pl.when(valid & (section == 0))(lambda: work(2))
    pl.when(valid & (section == 1))(lambda: work(0))

    @pl.when(jnp.logical_not(valid))
    def _():
        out[...] = jnp.zeros_like(out)


def decode(info, here, across, far, vectors, w_in, w_one, w_two):
    vmem = pl.BlockSpec(memory_space=pltpu.VMEM)
    hbm = pl.BlockSpec(memory_space=pl.ANY)
    tables = [w_in, *gathers()]
    return pl.pallas_call(
        decode_kernel,
        out_shape=jax.ShapeDtypeStruct((2, TS * TS, CH), BF16),
        in_specs=[pl.BlockSpec(memory_space=pltpu.SMEM)] + [vmem] * 8 + [hbm] * 7,
        out_specs=vmem,
        scratch_shapes=[pltpu.VMEM(t.shape, BF16) for t in tables]
        + [
            pltpu.VMEM((SPAN, STEM, EXT, EXT * ZC), BF16),
            pltpu.VMEM((SPAN, 5, 5, 16, CH), BF16),
            pltpu.VMEM((SPAN, 4, 4, 32, CH), BF16),
            pltpu.VMEM((2, 128, CH), F32),
            pltpu.VMEM((SPAN * MID_ROWS, CH), F32),
            pltpu.VMEM((3 * TAPS, CH), BF16),
            pltpu.VMEM((3 * TAPS, CH), BF16),
            pltpu.SemaphoreType.DMA((5,)),
            pltpu.SemaphoreType.DMA((2, 3)),
        ],
        compiler_params=pltpu.CompilerParams(vmem_limit_bytes=48 << 20),
        cost_estimate=pl.CostEstimate(
            flops=2 * 27 * CH * CH * (SPAN * MID_ROWS + 200), bytes_accessed=16 << 20, transcendentals=0
        ),
    )(info, here, across, far, *vectors, *tables, w_one, w_two)


def iota(shape, dim):
    return lax.broadcasted_iota(jnp.int32, shape, dim)


def slot_info(resolution, frame_counts, tile_rows, tile_cols, decoder_list, mine, width):
    shape = (6,) + decoder_list.shape
    which = iota(shape, 0)
    table = jnp.where(
        which == 0,
        tile_rows[None],
        jnp.where(
            which == 1,
            tile_cols[None],
            jnp.where(which == 2, resolution[None, :, None], frame_counts[None, :, None]),
        ),
    )
    picked = jnp.sum(jnp.where((decoder_list == mine)[None] & (which < 4), table, 0), axis=(1, 2))
    place = iota((6,), 0)
    return picked + jnp.where(place == 4, lax.axis_index("section"), jnp.where(place == 5, width, 0))


def local(
    latent, resolution, frame_counts, tile_rows, tile_cols, decoder_list,
    w_in, b_in, gain_one, w_one, b_one, gain_two, w_two, b_two,
):
    tiles = lax.axis_size("tile")
    video, tile = lax.axis_index("video"), lax.axis_index("tile")
    mine = video * tiles + tile
    flip = lambda a, by: lax.ppermute(a, "tile", [(i, i ^ by) for i in range(tiles)])
    unit = (2 * EXT, EXT * ZC)
    after = lambda done, *args: lax.optimization_barrier((done, *args))

    live = (tile < tiles // 2).astype(F32)
    got = [flip(latent, by) * live for by in (2, 6, 4)]
    have = jnp.concatenate([a.astype(BF16) for a in (latent, *got)]).reshape(8, *unit)
    have, named_by = after(have, decoder_list)
    have = jnp.concatenate([have, flip(have, 1)])

    shape = (8, 2) + decoder_list.shape
    step = iota(shape, 0)
    hop = (step >> 2) ^ ((step >> 1) & 1) * 6 ^ (step & 1) * 2
    here = (iota(shape, 2) == 2 * video + iota(shape, 1)) & (iota(shape, 3) == tile ^ hop)
    names = jnp.sum(jnp.where(here, named_by, 0), axis=(2, 3))

    shape = (8, 8, 2)
    row = iota(shape, 0)
    goal = mine ^ (row & 1) * tiles ^ ((row >> 1) & 1) * 24 ^ (row >> 2) * 8
    match = (goal == names[None]).reshape(8, 16)
    kept = jnp.sum(
        jnp.where(match[:, :, None, None], have[None], jnp.zeros((), BF16)), axis=1, dtype=F32
    ).astype(BF16)
    here = kept[:2] + flip(kept[6:], 16) + flip(kept[2:4], 24) + flip(kept[4:6], 8)
    around = lambda a, by: lax.ppermute(a, ("video", "section"), [(z, z ^ by) for z in range(4)])
    far = jnp.stack([around(here[1], 3), around(here[1], 2)])
    across = around(here[0], 1)

    _, resolution, frame_counts = after(kept, resolution, frame_counts)
    info = slot_info(
        resolution, frame_counts, tile_rows, tile_cols, decoder_list, mine, tiles // 4 * TS - 4
    )
    vectors = [b_in, gain_one, b_one, gain_two, b_two]
    return decode(info, here, across, far, vectors, w_in, w_one, w_two)[None, None]


def solution(mesh):
    return jax.shard_map(
        local,
        mesh=mesh,
        in_specs=(P("video", "tile", "section", None, None),) + (P(),) * 13,
        out_specs=P("video", "tile", "section", None, None),
        check_vma=False,
    )
```

```python
import jax
import jax.numpy as jnp
import numpy as np
from jax import lax
from jax.experimental import pallas as pl
from jax.experimental.pallas import tpu as pltpu
from jax.sharding import PartitionSpec as P

F32 = jnp.float32
BF16 = jnp.bfloat16
ZC = 16
CH = 384
EXT = 16
TS = 10
SPAN = 4
STEM = EXT - 2
MID = EXT - 4
STEM_ROWS = STEM * EXT
MID_ROWS = MID * MID
TAPS = 9 * CH


def gathers():
    one = np.zeros((25 * 16, STEM_ROWS), np.float32)
    for ry in range(5):
        for rx in range(5):
            for j in range(16):
                y, x = 3 * (j // 4) + ry, 3 * (j % 4) + rx
                one[(ry * 5 + rx) * 16 + j, x * EXT + y] = 1
    two = np.zeros((16 * 32, MID_ROWS), np.float32)
    for ry in range(4):
        for rx in range(4):
            for j in range(25):
                y, x = 2 * (j // 5) + ry, 2 * (j % 5) + rx
                two[(ry * 4 + rx) * 32 + j, ((y % 3) * 3 + x % 3) * 16 + (y // 3) * 4 + x // 3] = 1
    skip = np.zeros((4 * 32, STEM_ROWS), np.float32)
    out = np.zeros((112, 4 * 32), np.float32)
    for y in range(TS):
        for x in range(TS):
            row = ((y % 2) * 2 + x % 2) * 32 + (y // 2) * 5 + x // 2
            skip[row, (x + 2) * EXT + y + 2] = 1
            out[y * TS + x, row] = 1
    return [jnp.asarray(a, BF16) for a in (one, two, skip, out)]


def dot(a, b):
    return jnp.dot(a, b, preferred_element_type=F32)


def activate(u, gain):
    half = 0.5 * (u * lax.rsqrt(jnp.mean(u * u, axis=-1, keepdims=True) + 1e-06) * gain)
    return half + half * jnp.tanh(half)


def inside(row, col, high, wide):
    return ((row >= 0) & (row < high) & (col >= 0) & (col < wide)).astype(F32)


def decode_kernel(
    info, here, across, far, b_in, gain_one, b_one, gain_two, b_two, w_in_h, to_one_h, to_two_h, to_skip_h, to_out_h, w_one, w_two, out,
    w_in, to_one, to_two, to_skip, to_out, lhs, act_one, act_two, skip, middle, w_one_v, w_two_v, small, sems,
):
    row0, col0, high, count, section = info[0], info[1], (2 + 2 * info[2]) * TS - 3, info[3], info[4]
    wide, first = info[5], 2 * section - 2

    def taps(ref, start, frames, side, rows):
        return jnp.concatenate(
            [
                ref[start : start + frames, dy : dy + side, dx : dx + side].reshape(frames * rows, CH)
                for dy in range(3)
                for dx in range(3)
            ],
            axis=-1,
        )

    def work(low):
        known = SPAN - low
        tables = []
        for n, (src, dst) in enumerate(
            ((w_in_h, w_in), (to_one_h, to_one), (to_two_h, to_two), (to_skip_h, to_skip), (to_out_h, to_out))
        ):
            tables.append(pltpu.make_async_copy(src, dst, small.at[n]))
            tables[n].start()
        copies = {}
        for n, (src, dst) in enumerate(((w_one, w_one_v), (w_two, w_two_v))):
            for step in range(3):
                tap = 2 - step if n == 0 else step
                if tap == 0 and low:
                    continue
                copy = pltpu.make_async_copy(
                    src.at[pl.ds(tap * TAPS, TAPS)], dst.at[pl.ds(tap * TAPS, TAPS)], sems.at[n, tap]
                )
                copy.start()
                copies[n, tap] = copy
        bias_in, gain_1, bias_one, gain_2, bias_two = [
            v[...].reshape(1, CH) for v in (b_in, gain_one, b_one, gain_two, b_two)
        ]

        shape = (known * EXT, EXT * ZC)
        lane = lax.broadcasted_iota(jnp.int32, shape, 1)
        line = lax.broadcasted_iota(jnp.int32, shape, 0)
        cells = here[0].astype(F32) + far[1].astype(F32)
        if not low:
            other = across[...].astype(F32) + far[0].astype(F32)
            cells = jnp.concatenate([other, cells], axis=0)
        cells = cells * inside(row0 - 3 + (line & (EXT - 1)), col0 - 3 + lane // ZC, high, wide)
        rolled = [
            cells,
            pltpu.roll(pltpu.roll(cells, known * EXT - 1, 0), 3 * ZC, 1),
            pltpu.roll(pltpu.roll(cells, known * EXT - 2, 0), 6 * ZC, 1),
        ]
        for x in range(STEM):
            at = [pltpu.roll(r, EXT * ZC - ZC * x, 1) if x else r for r in rolled]
            packed = jnp.where(lane < 3 * ZC, at[0], jnp.where(lane < 6 * ZC, at[1], at[2]))
            lhs[low:SPAN, x] = packed.astype(BF16).reshape(known, EXT, EXT * ZC)

        for table in tables:
            table.wait()
        pos = lax.broadcasted_iota(jnp.int32, (STEM_ROWS, 1), 0)
        mask_one = inside(row0 - 2 + (pos & (EXT - 1)), col0 - 2 + (pos >> 4), high, wide)
        rows = lhs[low:SPAN].reshape(known * STEM_ROWS, EXT * ZC)[:, : 9 * ZC]
        part = {
            dt: dot(rows[: (known - 2 + dt) * STEM_ROWS], w_in[pl.ds(dt * 9 * ZC, 9 * ZC), :])
            for dt in range(3)
            if known - 2 + dt > 0
        }
        acts, skips = [], []
        for f in range(low, SPAN):
            stem = bias_in
            for dt in range(3):
                if f + dt - 2 >= low:
                    at = (f + dt - 2 - low) * STEM_ROWS
                    stem = stem + part[dt][at : at + STEM_ROWS]
            act = activate(stem, gain_1) * mask_one
            if f >= 2:
                coarse = stem.astype(BF16)
                fine = (stem - coarse.astype(F32)).astype(BF16)
                skips.append(jnp.concatenate([coarse, fine], axis=0))
            acts.append(act.astype(BF16))
        moved = dot(to_one[...], jnp.concatenate(acts, axis=1)).astype(BF16)
        for f in range(low, SPAN):
            act_one[f] = moved[:, (f - low) * CH : (f - low + 1) * CH].reshape(5, 5, 16, CH)
        twice = jnp.concatenate([to_skip[...], to_skip[...]], axis=1)
        moved = dot(twice, jnp.concatenate(skips, axis=1))
        for f in range(2):
            skip[f] = moved[:, f * CH : (f + 1) * CH] + bias_two

        for dt in (2, 1, 0):
            frames = known - 2 + dt
            if frames > 0:
                copies[0, dt].wait()
                add = dot(taps(act_one, low, frames, 3, MID_ROWS), w_one_v[pl.ds(dt * TAPS, TAPS), :])
                at = pl.ds((SPAN - frames) * MID_ROWS, frames * MID_ROWS)
                if dt == 2:
                    middle[at, :] = add
                else:
                    middle[at, :] += add
        spot = lax.broadcasted_iota(jnp.int32, (MID_ROWS, 1), 0)
        block = spot >> 4
        block_y = (block >= 3).astype(jnp.int32) + (block >= 6).astype(jnp.int32)
        mid_y = 3 * ((spot >> 2) & 3) + block_y
        mid_x = 3 * (spot & 3) + block - 3 * block_y
        mask_two = inside(row0 - 1 + mid_y, col0 - 1 + mid_x, high, wide)
        for f in range(low, SPAN):
            act = activate(middle[pl.ds(f * MID_ROWS, MID_ROWS), :] + bias_one, gain_2) * mask_two
            act_two[f] = dot(to_two[...], act.astype(BF16)).astype(BF16).reshape(4, 4, 32, CH)

        total = skip[...].reshape(2 * 128, CH)
        for dt in range(3):
            start = max(dt, low)
            if start > dt + 1:
                continue
            copies[1, dt].wait()
            frames = dt + 2 - start
            add = dot(taps(act_two, start, frames, 2, 128), w_two_v[pl.ds(dt * TAPS, TAPS), :])
            if frames == 1:
                add = jnp.concatenate([jnp.zeros((128, CH), F32), add], axis=0)
            total = total + add
        for f in range(2):
            live = first + 2 + f < count
            final = jnp.where(live, total[f * 128 : (f + 1) * 128], 0.0).astype(BF16)
            out[f] = dot(to_out[...], final)[: TS * TS].astype(BF16)

    valid = 2 * section < count
    pl.when(valid & (section == 0))(lambda: work(2))
    pl.when(valid & (section == 1))(lambda: work(0))

    @pl.when(jnp.logical_not(valid))
    def _():
        out[...] = jnp.zeros_like(out)


def decode(info, here, across, far, vectors, w_in, w_one, w_two):
    vmem = pl.BlockSpec(memory_space=pltpu.VMEM)
    hbm = pl.BlockSpec(memory_space=pl.ANY)
    tables = [w_in, *gathers()]
    return pl.pallas_call(
        decode_kernel,
        out_shape=jax.ShapeDtypeStruct((2, TS * TS, CH), BF16),
        in_specs=[pl.BlockSpec(memory_space=pltpu.SMEM)] + [vmem] * 8 + [hbm] * 7,
        out_specs=vmem,
        scratch_shapes=[pltpu.VMEM(t.shape, BF16) for t in tables]
        + [
            pltpu.VMEM((SPAN, STEM, EXT, EXT * ZC), BF16),
            pltpu.VMEM((SPAN, 5, 5, 16, CH), BF16),
            pltpu.VMEM((SPAN, 4, 4, 32, CH), BF16),
            pltpu.VMEM((2, 128, CH), F32),
            pltpu.VMEM((SPAN * MID_ROWS, CH), F32),
            pltpu.VMEM((3 * TAPS, CH), BF16),
            pltpu.VMEM((3 * TAPS, CH), BF16),
            pltpu.SemaphoreType.DMA((5,)),
            pltpu.SemaphoreType.DMA((2, 3)),
        ],
        compiler_params=pltpu.CompilerParams(vmem_limit_bytes=48 << 20),
        cost_estimate=pl.CostEstimate(
            flops=2 * 27 * CH * CH * (SPAN * MID_ROWS + 200), bytes_accessed=16 << 20, transcendentals=0
        ),
    )(info, here, across, far, *vectors, *tables, w_one, w_two)


def iota(shape, dim):
    return lax.broadcasted_iota(jnp.int32, shape, dim)


def slot_info(resolution, frame_counts, tile_rows, tile_cols, decoder_list, mine, width):
    shape = (6,) + decoder_list.shape
    which = iota(shape, 0)
    table = jnp.where(
        which == 0,
        tile_rows[None],
        jnp.where(
            which == 1,
            tile_cols[None],
            jnp.where(which == 2, resolution[None, :, None], frame_counts[None, :, None]),
        ),
    )
    picked = jnp.sum(jnp.where((decoder_list == mine)[None] & (which < 4), table, 0), axis=(1, 2))
    place = iota((6,), 0)
    return picked + jnp.where(place == 4, lax.axis_index("section"), jnp.where(place == 5, width, 0))


def local(
    latent, resolution, frame_counts, tile_rows, tile_cols, decoder_list,
    w_in, b_in, gain_one, w_one, b_one, gain_two, w_two, b_two,
):
    tiles = lax.axis_size("tile")
    video, tile = lax.axis_index("video"), lax.axis_index("tile")
    mine = video * tiles + tile
    flip = lambda a, by: lax.ppermute(a, "tile", [(i, i ^ by) for i in range(tiles)])
    unit = (2 * EXT, EXT * ZC)
    after = lambda done, *args: lax.optimization_barrier((done, *args))

    live = (tile < tiles // 2).astype(F32)
    got = [flip(latent, by) * live for by in (6, 2, 4)]
    have = jnp.concatenate([a.astype(BF16) for a in (latent, *got)]).reshape(8, *unit)
    have, named_by = after(have, decoder_list)
    have = jnp.concatenate([have, flip(have, 1)])

    shape = (8, 2) + decoder_list.shape
    step = iota(shape, 0)
    hop = (step >> 2) ^ ((step >> 1) & 1) * 2 ^ (step & 1) * 6
    here = (iota(shape, 2) == 2 * video + iota(shape, 1)) & (iota(shape, 3) == tile ^ hop)
    names = jnp.sum(jnp.where(here, named_by, 0), axis=(2, 3))

    shape = (8, 8, 2)
    row = iota(shape, 0)
    goal = mine ^ (row & 1) * tiles ^ ((row >> 1) & 1) * 24 ^ (row >> 2) * 8
    match = (goal == names[None]).reshape(8, 16)
    kept = jnp.sum(
        jnp.where(match[:, :, None, None], have[None], jnp.zeros((), BF16)), axis=1, dtype=F32
    ).astype(BF16)
    here = kept[:2] + flip(kept[6:], 16) + flip(kept[2:4], 24) + flip(kept[4:6], 8)
    around = lambda a, by: lax.ppermute(a, ("video", "section"), [(z, z ^ by) for z in range(4)])
    far = jnp.stack([around(here[1], 3), around(here[1], 2)])
    across = around(here[0], 1)

    _, resolution, frame_counts = after(kept, resolution, frame_counts)
    info = slot_info(
        resolution, frame_counts, tile_rows, tile_cols, decoder_list, mine, tiles // 4 * TS - 4
    )
    vectors = [b_in, gain_one, b_one, gain_two, b_two]
    return decode(info, here, across, far, vectors, w_in, w_one, w_two)[None, None]


def solution(mesh):
    return jax.shard_map(
        local,
        mesh=mesh,
        in_specs=(P("video", "tile", "section", None, None),) + (P(),) * 13,
        out_specs=P("video", "tile", "section", None, None),
        check_vma=False,
    )
```
